256 devices in a mesh: sample: 32 (over z, x_hi, core), feat: 8 (over x_lo, y).
Axes of the slice: x: 4 (x_hi: 2, x_lo: 2; x = x_hi * 2 + x_lo), y: 4, z: 8, core: 2. Of those that a mesh axis runs over, the one named last changes fastest.
Arguments:
- expression: bfloat16 [8192, 65536], P('sample', 'feat'), may hold values from -6 to 6
- factors: float32 [8192, 256], P('sample'), may hold values from -1.5 to 1.5
- loadings: float32 [65536, 256], P(('feat', 'sample')), may hold values from -1.5 to 1.5
- batch_mask: int32 [2, 5], replicated, may hold values 0 or 1
- modality: int32 [65536], P('feat'), may hold values from 0 to 4, as said below
Outputs:
- factors_out: float32 [8192, 256], P('sample')
- loadings_out: float32 [65536, 256], P(('feat', 'sample'))
The draws below stay inside these ranges and needn't reach their ends.
Inputs may be any that keep to these rules, and one draw needn't show every extreme that they name: `modality`: modalities 0 to 4 hold 2048, 4096, 6144, 16384 and 36864 features, in a random order.
All inputs are finite; a program needn't handle non-finite values.
Results may differ from the reference program's by a relative error of at most 0.0031.
Values may be sent and summed in bfloat16 or wider, within the bound.
A program may use at most 128 MiB of HBM per device.

```python
import math
import jax
import jax.numpy as jnp
from jax import lax

K = 256
F = 65536
MODS = 5
BATCH = 4096
ITERS = 2
C = 256
CELLS = 8192
NB = 2
N_SAMPLE = 32


def draw_modality(key, part):
    key = jax.random.fold_in(key, 11)
    index = jnp.arange(F, dtype=jnp.int32) * 32
    layout = jnp.zeros((F,), jnp.int32)
    for bound in (1, 3, 6, 14):
        layout = layout + (index >= bound * F).astype(jnp.int32)
    return jax.random.permutation(key, layout)


def set_ends(entries, key, least, high):
    longest = entries.shape.index(max(entries.shape))
    spots = []
    for shift in (0, 1):
        where = [jax.random.randint(jax.random.fold_in(key, axis), (), 0, length) for axis, length in enumerate(entries.shape)]
        where[longest] = (where[longest] + shift) % entries.shape[longest]
        spots.append(tuple(where))
    return entries.at[spots[0]].set(least).at[spots[1]].set(high)


def spiked(values, key, source, target, shards_of, factor):
    def block_of(axis_at):
        return (jnp.arange(values.shape[axis_at]) // (values.shape[axis_at] // shards_of)).reshape((-1,) + (1,) * (values.ndim - 1 - axis_at))

    one_side = jax.random.permutation(key, shards_of)[block_of(target)]
    far = (block_of(target) + shards_of // 2) % shards_of
    return jnp.where((block_of(source) == one_side) | (block_of(source) == far), factor * values, values)


def levels(key, dims, shards, least, top_value):
    level = 1.0
    for axis_at, blocks in shards:
        steps = jax.random.uniform(jax.random.fold_in(jax.random.fold_in(key, 6), axis_at), (blocks,), jnp.float32, least / len(shards), top_value / len(shards))
        level = level * jnp.repeat(jnp.exp(steps), dims[axis_at] // blocks).reshape((-1,) + (1,) * (len(dims) - 1 - axis_at))
    return level


def centred(own_key, dims, width, most, pieces=(), kind=jnp.bfloat16):
    gain = levels(own_key, dims, pieces, -0.22, 0.18) if pieces else 1.0
    values = jax.random.normal(own_key, dims, jnp.float32) * width * gain
    return jnp.minimum(jnp.maximum(values, -most), most).astype(kind)


def gaussian_with(stream_key, extent, spread, limit, split, heavy, kind=jnp.bfloat16):
    array = spread * jax.random.normal(stream_key, extent, jnp.float32)
    if split:
        array = array * levels(stream_key, extent, split, -0.22, 0.18)
    return jnp.clip(spiked(array, jax.random.fold_in(stream_key, 3), *heavy), -limit, limit).astype(kind)


def setup_inputs(seed: int = 0) -> dict:
    seeds = jax.random.split(jax.random.key(seed), 6)
    expression = gaussian_with(seeds[0], (CELLS, F), 1.0, 6.0, ((0, 32), (1, 8)), (0, 1, 32, 2.75))
    factors = centred(seeds[1], (CELLS, K), 0.25, 1.5, ((0, 32),), jnp.float32)
    loadings = centred(seeds[2], (F, K), 0.25, 1.5, ((0, 256),), jnp.float32)
    batch_mask = set_ends((jax.random.randint(seeds[3], (NB, MODS), 0, 3) < 2).astype(jnp.int32), jax.random.fold_in(seeds[3], 1), 0, 1)
    modality = draw_modality(jax.random.fold_in(seeds[5], 71), 0)
    return dict(expression=expression, factors=factors, loadings=loadings, batch_mask=batch_mask, modality=modality)


def reference(expression, factors, loadings, batch_mask, modality):
    cells = C * N_SAMPLE
    rate_z = 0.9 * math.sqrt(K) / F
    rate_w = 0.9 * math.sqrt(K) / cells
    onehot = (modality[:, None] == jnp.arange(MODS, dtype=jnp.int32)[None, :]).astype(jnp.float32)
    table = lax.optimization_barrier(jnp.sum(batch_mask.astype(jnp.float32)[:, None, :] * onehot[None, :, :], axis=2))
    for step in range(ITERS):
        wb = loadings.astype(jnp.bfloat16)
        zb = factors.astype(jnp.bfloat16)

        def block(total, index):
            first = (index * C).astype(jnp.int32)
            rows = lax.dynamic_slice_in_dim(zb, first, C, 0)
            data = lax.dynamic_slice_in_dim(expression, first, C, 0)
            which = (first // BATCH).astype(jnp.int32)
            seen = lax.dynamic_slice_in_dim(table, which, 1, 0)
            pred = lax.dot_general(rows, wb, (((1,), (1,)), ((), ())), preferred_element_type=jnp.float32)
            resid = (seen * (pred - data.astype(jnp.float32))).astype(jnp.bfloat16)
            grad_rows = jnp.dot(resid, wb, preferred_element_type=jnp.float32)
            total = total + lax.dot_general(resid, rows, (((0,), (0,)), ((), ())), preferred_element_type=jnp.float32)
            return (total, grad_rows)
        grad_w, grad_z = lax.scan(block, jnp.zeros((F, K), jnp.float32), jnp.arange(N_SAMPLE, dtype=jnp.int32))
        grad_z = grad_z.reshape(cells, K)
        factors = factors - rate_z * grad_z
        loadings = loadings - rate_w * grad_w
    return (factors, loadings)
```

```python
import math

import jax
import jax.numpy as jnp
from jax import lax
from jax.experimental import pallas as pl
from jax.experimental.pallas import tpu as pltpu
from jax.sharding import PartitionSpec as P

ITERS = 2
NZ = 8
NF = 8
T = 256
MODS = 5
BF = jnp.bfloat16
F32 = jnp.float32
STREAMS = ((0, 0), (1, 1), (0, 1), (1, 0))
FULL = ((0, 0), (1, 1))


def nn(a, b):
    return jnp.dot(a, b, preferred_element_type=F32)


def nt(a, b):
    return lax.dot_general(a, b, (((1,), (1,)), ((), ())), preferred_element_type=F32)


def kernel(
    rate_z, rate_w,
    x_hbm, z_in, w_in, mask, modality, z_out, w_out,
    x, obs, zb, zt, zf, wf, wg, own, sib_out, sib_in, ring_out, ring_in, pair_out, pair_in,
    g_local, g_sib, g_half, g_pair, g_z, g_all, pz, z_in_parts, z_new,
    x_sem, ag_s, ag_r, agx_s, agx_r, ags_s, ags_r, rs_s, rs_r, rsx_s, rsx_r, rss_s, rss_r,
    g_s, g_r, gz_s, gz_r, gf_s, gf_r, az_s, az_r, an_s, an_r,
):
    s = lax.axis_index("sample")
    k = lax.axis_index("feat")
    z = s // 4
    xh = (s // 2) % 2
    c = s % 2
    batch = z // 4
    sibling = {"sample": z * 4 + xh * 2 + (1 - c)}
    partner = {"sample": z * 4 + (1 - xh) * 2 + c}

    def along(step):
        return {"sample": ((z + step + NZ) % NZ) * 4 + xh * 2 + c}

    def peer(off):
        return {"feat": (k + off) % NF}

    neighbour = (along(1), along(-1))
    started = []

    def copy(src, dst, send, recv, device):
        return pltpu.make_async_remote_copy(
            src_ref=src, dst_ref=dst, send_sem=send, recv_sem=recv,
            device_id=device, device_id_type=pl.DeviceIdType.MESH,
        )

    def send(*args):
        one = copy(*args)
        one.start()
        started.append(one)

    def shard(rel_z, col, core):
        which = xh if col == 0 else 1 - xh
        return ((z + rel_z + NZ) % NZ) * 4 + which * 2 + core

    load_x = pltpu.make_async_copy(x_hbm, x, x_sem)
    load_x.start()
    zb[0] = z_in[...].astype(BF)
    wf[0] = w_in[...]
    wg[0, s] = w_in[...].astype(BF)

    barrier = pltpu.get_barrier_semaphore()
    greet = [sibling, partner] + [along(d) for d in range(1, NZ)] + [peer(d) for d in range(1, NF)]
    for device in greet:
        pl.semaphore_signal(barrier, inc=1, device_id=device, device_id_type=pl.DeviceIdType.MESH)
    pl.semaphore_wait(barrier, len(greet))

    def ag_hop(it, d, col, t):
        return (d, col) in FULL or t < 3

    def ag_send(it, d, col, t):
        origin = shard(-t if d == 0 else t, col, c)
        block = wg.at[it, origin]
        i = ((it * 2 + d) * 2 + col) * 4 + t
        send(block, block, ag_s.at[i], ag_r.at[i], neighbour[d])

    def ag_sibling(it, rel, col):
        block = wg.at[it, shard(rel, col, c)]
        i = (it * NZ + rel % NZ) * 2 + col
        send(block, block, ags_s.at[i], ags_r.at[i], sibling)

    def ag_begin(it):
        for d in (0, 1):
            ag_send(it, d, 0, 0)
        block = wg.at[it, s]
        send(block, block, agx_s.at[it], agx_r.at[it], partner)
        ag_sibling(it, 0, 0)

    def ag_pair(it):
        block = wg.at[it, shard(0, 1, c)]
        copy(block, block, agx_s.at[it], agx_r.at[it], partner).wait_recv()
        for d in (0, 1):
            ag_send(it, d, 1, 0)
        ag_sibling(it, 0, 1)

    def ag_step(it, t):
        for d, col in ((0, 0), (1, 0), (0, 1), (1, 1)):
            if not ag_hop(it, d, col, t):
                continue
            rel = -(t + 1) if d == 0 else t + 1
            block = wg.at[it, shard(rel, col, c)]
            i = ((it * 2 + d) * 2 + col) * 4 + t
            copy(block, block, ag_s.at[i], ag_r.at[i], neighbour[d]).wait_recv()
            if t < 3 and ag_hop(it, d, col, t + 1):
                ag_send(it, d, col, t + 1)
            ag_sibling(it, rel % NZ, col)

    def ag_from_sibling(it, rel):
        for col in (0, 1):
            block = wg.at[it, shard(rel, col, 1 - c)]
            i = (it * NZ + rel % NZ) * 2 + col
            copy(block, block, ags_s.at[i], ags_r.at[i], sibling).wait_recv()

    def factor_part(it, rel, first=False):
        ag_from_sibling(it, rel)
        there = (z + rel + NZ) % NZ

        def body(j, carry):
            w = wg[it, pl.ds(there * 4 + j * 2, 2)].reshape(2 * T, T)
            cols = pl.ds(pl.multiple_of(there * 4 * T + j * 2 * T, 2 * T), 2 * T)
            pred = nt(zb[it], w)
            resid = (obs[batch, :, cols] * (pred - x[:, cols].astype(F32))).astype(BF)
            pz[it] += nn(resid, w)
            return carry

        if first:
            pz[it] = jnp.zeros((T, T), F32)
        lax.fori_loop(0, 2, body, 0)

    def cross(it, low, high):
        def body(i, carry):
            odd = i % 2
            rel = (4 + i // 2 - odd * (2 * (i // 2) + 1)) % NZ
            there = (z + rel) % NZ
            for col in (0, 1):
                which = xh if col == 0 else 1 - xh
                for mine in (False, True):
                    core = c if mine else 1 - c
                    cols = pl.ds(pl.multiple_of((there * 4 + which * 2 + core) * T, T), T)
                    value = nn(zt[...], x[:, cols]) * obs[batch, :, cols]
                    slot = rel * 2 + col
                    if mine:
                        own[slot] = value
                    else:
                        sib_out[it, slot] = value.astype(BF)
                        sem = it * 2 * NZ + slot
                        copy(
                            sib_out.at[it, slot], sib_in.at[it, slot], rss_s.at[sem], rss_r.at[sem], sibling
                        ).start()
            return carry

        lax.fori_loop(low, high, body, 0)

    def cross_end(it):
        def body(slot, carry):
            sem = it * 2 * NZ + slot
            copy(
                sib_out.at[it, slot], sib_in.at[it, slot], rss_s.at[sem], rss_r.at[sem], sibling
            ).wait_send()
            return carry

        lax.fori_loop(0, 2 * NZ, body, 0)

    def chip_sum(it, rel, col):
        slot = (rel % NZ) * 2 + col
        sem = it * 2 * NZ + slot
        copy(
            sib_out.at[it, slot], sib_in.at[it, slot], rss_s.at[sem], rss_r.at[sem], sibling
        ).wait_recv()
        return own[slot] + sib_in[it, slot].astype(F32)

    def arrived(it, d, col, t):
        i = ((it * 2 + d) * 2 + col) * 4 + t
        copy(ring_out.at[i], ring_in.at[i], rs_s.at[i], rs_r.at[i], neighbour[d]).wait_recv()
        return ring_in[i].astype(F32)

    def rs_step(it, t):
        for d, col in STREAMS:
            if t == 0 and (d, col) not in FULL:
                continue
            value = chip_sum(it, 4 - t if d == 0 else t - 4, col)
            if t > 1 or (t == 1 and (d, col) in FULL):
                value = value + arrived(it, d, col, t - 1)
            i = ((it * 2 + d) * 2 + col) * 4 + t
            ring_out[i] = value.astype(BF)
            send(ring_out.at[i], ring_in.at[i], rs_s.at[i], rs_r.at[i], neighbour[d])

    def rs_pair_send(it):
        value = chip_sum(it, 0, 1) + arrived(it, 0, 1, 3) + arrived(it, 1, 1, 3)
        pair_out[it] = value.astype(BF)
        send(pair_out.at[it], pair_in.at[it], rsx_s.at[it], rsx_r.at[it], partner)

    def rs_end(it):
        value = chip_sum(it, 0, 0) + arrived(it, 0, 0, 3) + arrived(it, 1, 0, 3)
        copy(pair_out.at[it], pair_in.at[it], rsx_s.at[it], rsx_r.at[it], partner).wait_recv()
        return value + pair_in[it].astype(F32)

    half = pl.multiple_of(k * 32 + c * 16, 16)
    other_half = pl.multiple_of(k * 32 + (1 - c) * 16, 16)
    base = pl.multiple_of(k * 32 + c * 16 + xh * 8, 8)
    mine8 = pl.multiple_of(xh * 8, 8)
    other8 = pl.multiple_of((1 - xh) * 8, 8)

    def gram(it):
        zt[...] = zb[it].astype(F32).T.astype(BF)
        g_local[it] = nn(zt[...], zb[it])
        i = it * 4
        send(g_local.at[it, pl.ds(other_half, 16)], g_sib.at[it], g_s.at[i], g_r.at[i], sibling)

    def gram_pair(it):
        i = it * 4
        copy(g_half.at[it], g_sib.at[it], g_s.at[i], g_r.at[i], sibling).wait_recv()
        g_half[it] = g_local[it, pl.ds(half, 16)] + g_sib[it]
        i = it * 4 + 1
        send(g_half.at[it, pl.ds(other8, 8)], g_pair.at[it], g_s.at[i], g_r.at[i], partner)

    def gram_z(it):
        i = it * 4 + 1
        copy(g_pair.at[it], g_pair.at[it], g_s.at[i], g_r.at[i], partner).wait_recv()
        g_z[it, z] = g_half[it, pl.ds(mine8, 8)] + g_pair[it]
        for off in range(1, NZ):
            i = it * NZ + off
            send(g_z.at[it, z], g_z.at[it, z], gz_s.at[i], gz_r.at[i], along(off))

    def gram_batches(it):
        for off in range(1, NZ):
            i = it * NZ + off
            slot = g_z.at[it, (z + NZ - off) % NZ]
            copy(slot, slot, gz_s.at[i], gz_r.at[i], along(off)).wait_recv()
        for b in (0, 1):
            g_all[it, b, pl.ds(base, 8)] = (
                (g_z[it, 4 * b] + g_z[it, 4 * b + 1]) + (g_z[it, 4 * b + 2] + g_z[it, 4 * b + 3])
            )
        block = g_all.at[it, :, pl.ds(base, 8)]
        send(block, block, g_s.at[it * 4 + 2], g_r.at[it * 4 + 2], partner)

    def gram_sibling(it):
        rows = pl.multiple_of(k * 32 + c * 16 + (1 - xh) * 8, 8)
        block = g_all.at[it, :, pl.ds(rows, 8)]
        copy(block, block, g_s.at[it * 4 + 2], g_r.at[it * 4 + 2], partner).wait_recv()
        block = g_all.at[it, :, pl.ds(half, 16)]
        send(block, block, g_s.at[it * 4 + 3], g_r.at[it * 4 + 3], sibling)

    def gram_feat(it):
        block = g_all.at[it, :, pl.ds(other_half, 16)]
        copy(block, block, g_s.at[it * 4 + 3], g_r.at[it * 4 + 3], sibling).wait_recv()
        block = g_all.at[it, :, pl.ds(pl.multiple_of(k * 32, 32), 32)]
        for off in range(1, NF):
            i = it * NF + off
            send(block, block, gf_s.at[i], gf_r.at[i], peer(off))

    def new_loadings(it):
        for off in range(1, NF):
            i = it * NF + off
            rows = pl.multiple_of(((k + NF - off) % NF) * 32, 32)
            block = g_all.at[it, :, pl.ds(rows, 32)]
            copy(block, block, gf_s.at[i], gf_r.at[i], peer(off)).wait_recv()
        cols = pl.ds(pl.multiple_of(s * T, T), T)
        w = wg[it, s]
        grad = jnp.zeros((T, T), F32)
        for b in (0, 1):
            g = g_all[it, b]
            high = g.astype(BF)
            low = (g - high.astype(F32)).astype(BF)
            grad = grad + obs[b, :, cols] * (nt(high, w) + nt(low, w))
        grad = grad - rs_end(it)
        return wf[it] - rate_w * grad.T

    rows32 = pl.multiple_of(k * 32, 32)

    def factors_send(it):
        for off in range(1, NF):
            i = it * NF + off
            rows = pl.multiple_of(((k + off) % NF) * 32, 32)
            send(pz.at[it, pl.ds(rows, 32)], z_in_parts.at[it, off], az_s.at[i], az_r.at[i], peer(off))

    def factors_sum(it):
        total = pz[it, pl.ds(rows32, 32)]
        for off in range(1, NF):
            i = it * NF + off
            slot = z_in_parts.at[it, off]
            copy(slot, slot, az_s.at[i], az_r.at[i], peer(off)).wait_recv()
            total = total + z_in_parts[it, off]
        old = z_in[pl.ds(rows32, 32)] if it == 0 else zf[...]
        new = old - rate_z * total
        if it == 0:
            zf[...] = new
            zb[1, pl.ds(rows32, 32)] = new.astype(BF)
        else:
            z_new[pl.ds(rows32, 32)] = new
        target = zb.at[1] if it == 0 else z_new
        block = target.at[pl.ds(rows32, 32)]
        for off in range(1, NF):
            i = it * NF + off
            send(block, block, an_s.at[i], an_r.at[i], peer(off))

    def factors_wait(it):
        target = zb.at[1] if it == 0 else z_new
        for off in range(1, NF):
            i = it * NF + off
            block = target.at[pl.ds(pl.multiple_of(((k + NF - off) % NF) * 32, 32), 32)]
            copy(block, block, an_s.at[i], an_r.at[i], peer(off)).wait_recv()

    for it in range(ITERS):
        if it == 0:
            ag_begin(0)
            gram(0)
            for b in (0, 1):
                seen = jnp.zeros(modality.shape, F32)
                for m in range(MODS):
                    seen = jnp.where(modality[...] == m, mask[b, m].astype(F32), seen)
                obs[b] = seen
            load_x.wait()
        else:
            factors_sum(0)
            ag_pair(1)
            factors_wait(0)
            gram(1)
        cross(it, 0, 3)
        rs_step(it, 0)
        if it == 0:
            ag_pair(0)
        gram_pair(it)
        cross(it, 3, NZ)
        gram_z(it)
        rs_step(it, 1)
        ag_step(it, 0)
        factor_part(it, 0, first=True)
        gram_batches(it)
        rs_step(it, 2)
        ag_step(it, 1)
        gram_sibling(it)
        factor_part(it, 1)
        factor_part(it, 7)
        rs_step(it, 3)
        ag_step(it, 2)
        gram_feat(it)
        factor_part(it, 2)
        factor_part(it, 6)
        rs_pair_send(it)
        ag_step(it, 3)
        factor_part(it, 3)
        factor_part(it, 5)
        new = new_loadings(it)
        if it == 0:
            wf[1] = new
            wg[1, s] = new.astype(BF)
            ag_begin(1)
            factor_part(it, 4)
            factors_send(it)
        else:
            w_out[...] = new
            factor_part(it, 4)
            factors_send(it)
            factors_sum(it)
            factors_wait(it)
            z_out[...] = z_new[...]

    for one in started:
        one.wait_send()
    for it in range(ITERS):
        cross_end(it)


def per_device(expression, factors, loadings, batch_mask, modality):
    rows = factors.shape[0]
    rank = factors.shape[1]
    cells = rows * lax.axis_size("sample")
    width = expression.shape[1]
    features = width * lax.axis_size("feat")
    rate_z = 0.9 * math.sqrt(rank) / features
    rate_w = 0.9 * math.sqrt(rank) / cells
    vm = pl.BlockSpec(memory_space=pltpu.VMEM)
    dma = lambda n: pltpu.SemaphoreType.DMA((n,))
    out = jax.ShapeDtypeStruct((T, T), F32)

    def body(*refs):
        kernel(rate_z, rate_w, *refs)

    return pl.pallas_call(
        body,
        out_shape=(out, out),
        in_specs=[
            pl.BlockSpec(memory_space=pl.ANY), vm, vm, pl.BlockSpec(memory_space=pltpu.SMEM), vm,
        ],
        out_specs=(vm, vm),
        scratch_shapes=[
            pltpu.VMEM((rows, width), BF),
            pltpu.VMEM((2, 1, width), F32),
            pltpu.VMEM((ITERS, T, T), BF),
            pltpu.VMEM((T, T), BF),
            pltpu.VMEM((32, T), F32),
            pltpu.VMEM((ITERS, T, T), F32),
            pltpu.VMEM((ITERS, 32, T, T), BF),
            pltpu.VMEM((2 * NZ, T, T), F32),
            pltpu.VMEM((ITERS, 2 * NZ, T, T), BF),
            pltpu.VMEM((ITERS, 2 * NZ, T, T), BF),
            pltpu.VMEM((ITERS * 16, T, T), BF),
            pltpu.VMEM((ITERS * 16, T, T), BF),
            pltpu.VMEM((ITERS, T, T), BF),
            pltpu.VMEM((ITERS, T, T), BF),
            pltpu.VMEM((ITERS, T, T), F32),
            pltpu.VMEM((ITERS, 16, T), F32),
            pltpu.VMEM((ITERS, 16, T), F32),
            pltpu.VMEM((ITERS, 8, T), F32),
            pltpu.VMEM((ITERS, NZ, 8, T), F32),
            pltpu.VMEM((ITERS, 2, T, T), F32),
            pltpu.VMEM((ITERS, T, T), F32),
            pltpu.VMEM((ITERS, NF, 32, T), F32),
            pltpu.VMEM((T, T), F32),
            pltpu.SemaphoreType.DMA,
            dma(ITERS * 16), dma(ITERS * 16),
            dma(ITERS), dma(ITERS),
            dma(ITERS * 16), dma(ITERS * 16),
            dma(ITERS * 16), dma(ITERS * 16),
            dma(ITERS), dma(ITERS),
            dma(ITERS * 16), dma(ITERS * 16),
            dma(ITERS * 4), dma(ITERS * 4),
            dma(ITERS * NZ), dma(ITERS * NZ),
            dma(ITERS * NF), dma(ITERS * NF),
            dma(ITERS * NF), dma(ITERS * NF),
            dma(ITERS * NF), dma(ITERS * NF),
        ],
        compiler_params=pltpu.CompilerParams(
            collective_id=0, has_side_effects=True, vmem_limit_bytes=60 * 1024 * 1024
        ),
    )(expression, factors, loadings, batch_mask, modality.reshape(1, width))


def solution(mesh):
    return jax.shard_map(
        per_device,
        mesh=mesh,
        in_specs=(
            P("sample", "feat"),
            P("sample", None),
            P(("feat", "sample"), None),
            P(),
            P("feat"),
        ),
        out_specs=(P("sample", None), P(("feat", "sample"), None)),
        check_vma=False,
    )
```

```python
import math

import jax
import jax.numpy as jnp
from jax import lax
from jax.experimental import pallas as pl
from jax.experimental.pallas import tpu as pltpu
from jax.sharding import PartitionSpec as P

ITERS = 2
NZ = 8
NF = 8
T = 256
MODS = 5
BF = jnp.bfloat16
F32 = jnp.float32
H = T // 2
KINDS = ((0, 0), (0, 1), (1, 1))
AG_FULL = ((0, 0), (0, 1), (1, 2))
RS_FULL = ((1, 0), (1, 1), (0, 2))
ORDER = (
    ("agb", 0), ("gram", 0), ("ld",), ("cr", 0, 4), ("cr", 0, 3), ("cr", 0, 5), ("cr", 0, 2), ("agp", 0),
    ("rs", 0, 1, 1, 0), ("rx", 0, 4), ("rs", 0, 0, 2, 0), ("ag", 0, 0, 0, 0), ("ag", 0, 1, 0, 0),
    ("rs", 0, 0, 1, 1), ("rx", 0, 3), ("cr", 0, 6), ("ag", 0, 0, 1, 0), ("ag", 0, 1, 1, 0), ("rx", 0, 5),
    ("rs", 0, 1, 2, 1), ("cr", 0, 1), ("rx", 0, 2), ("rs", 0, 1, 0, 0), ("ag", 0, 0, 2, 0), ("ag", 0, 1, 2, 0),
    ("cr", 0, 7), ("cr", 0, 0), ("rx", 0, 6), ("rs", 0, 0, 2, 1), ("rs", 0, 1, 1, 1), ("gp", 0), ("agc", 0, 0),
    ("agc", 0, 7), ("agc", 0, 1), ("ag", 0, 0, 0, 1), ("ag", 0, 1, 0, 1), ("rx", 0, 1), ("rs", 0, 0, 0, 1),
    ("ag", 0, 1, 1, 1), ("rs", 0, 0, 1, 2), ("rx", 0, 7), ("rx", 0, 0), ("ag", 0, 0, 1, 1), ("rs", 0, 1, 2, 2),
    ("fp", 0, 0), ("ag", 0, 0, 2, 1), ("rs", 0, 1, 0, 1), ("fp", 0, 7), ("ag", 0, 1, 2, 1), ("rs", 0, 0, 2, 2),
    ("gz", 0), ("fp", 0, 1), ("ag", 0, 0, 0, 2), ("rs", 0, 1, 1, 2), ("agc", 0, 6), ("ag", 0, 1, 0, 2),
    ("rs", 0, 0, 0, 2), ("agc", 0, 2), ("fp", 0, 6), ("ag", 0, 1, 1, 2), ("rs", 0, 0, 1, 3), ("fp", 0, 2),
    ("ag", 0, 0, 1, 2), ("rs", 0, 1, 2, 3), ("ag", 0, 0, 2, 2), ("rs", 0, 1, 0, 2), ("agc", 0, 5),
    ("ag", 0, 1, 2, 2), ("rs", 0, 0, 2, 3), ("gb", 0), ("fp", 0, 5), ("agc", 0, 3), ("ag", 0, 0, 0, 3),
    ("rs", 0, 1, 1, 3), ("gs", 0), ("fp", 0, 3), ("rs", 0, 0, 0, 3), ("gf", 0), ("rs", 0, 1, 0, 3),
    ("agc", 0, 4), ("ag", 0, 0, 1, 3), ("ag", 0, 1, 2, 3), ("rp", 0), ("fp", 0, 4), ("fs", 0), ("nl", 0),
    ("agb", 1), ("fsum", 0), ("agp", 1), ("ag", 1, 0, 0, 0), ("ag", 1, 1, 0, 0), ("agc", 1, 0), ("fw", 0),
    ("gram", 1), ("ag", 1, 0, 1, 0), ("ag", 1, 1, 1, 0), ("fp", 1, 0), ("ag", 1, 0, 2, 0), ("ag", 1, 1, 2, 0),
    ("agc", 1, 7), ("gp", 1), ("cr", 1, 4), ("cr", 1, 3), ("ag", 1, 0, 0, 1), ("ag", 1, 1, 0, 1), ("fp", 1, 7),
    ("ag", 1, 0, 1, 1), ("ag", 1, 1, 1, 1), ("gz", 1), ("rx", 1, 4), ("rx", 1, 3), ("ag", 1, 0, 2, 1),
    ("ag", 1, 1, 2, 1), ("rs", 1, 1, 1, 0), ("rs", 1, 0, 2, 0), ("rs", 1, 0, 1, 1), ("agc", 1, 1),
    ("agc", 1, 6), ("ag", 1, 0, 0, 2), ("ag", 1, 1, 0, 2), ("agc", 1, 2), ("cr", 1, 5), ("fp", 1, 1),
    ("ag", 1, 0, 1, 2), ("ag", 1, 1, 1, 2), ("fp", 1, 6), ("gb", 1), ("ag", 1, 0, 2, 2), ("ag", 1, 1, 2, 2),
    ("rx", 1, 5), ("fp", 1, 2), ("rs", 1, 1, 0, 0), ("rs", 1, 0, 0, 1), ("rs", 1, 1, 2, 1), ("rs", 1, 0, 2, 1),
    ("gs", 1), ("rs", 1, 1, 1, 1), ("agc", 1, 5), ("agc", 1, 3), ("cr", 1, 2), ("cr", 1, 6),
    ("ag", 1, 0, 0, 3), ("ag", 1, 1, 2, 3), ("fp", 1, 5), ("ag", 1, 0, 1, 3), ("fp", 1, 3), ("rx", 1, 2),
    ("rx", 1, 6), ("rs", 1, 1, 0, 1), ("rs", 1, 0, 1, 2), ("rs", 1, 1, 2, 2), ("gf", 1), ("rs", 1, 0, 2, 2),
    ("rs", 1, 1, 1, 2), ("agc", 1, 4), ("cr", 1, 1), ("cr", 1, 7), ("rs", 1, 0, 0, 2), ("fp", 1, 4), ("fs", 1),
    ("rx", 1, 1), ("rs", 1, 1, 0, 2), ("rs", 1, 0, 1, 3), ("cr", 1, 0), ("rx", 1, 7), ("rs", 1, 1, 2, 3),
    ("rs", 1, 0, 2, 3), ("rs", 1, 1, 1, 3), ("rx", 1, 0), ("rs", 1, 0, 0, 3), ("rs", 1, 1, 0, 3), ("fsum", 1),
    ("rp", 1), ("nl", 1), ("fw", 1),
)


def nn(a, b):
    return jnp.dot(a, b, preferred_element_type=F32)


def nt(a, b):
    return lax.dot_general(a, b, (((1,), (1,)), ((), ())), preferred_element_type=F32)


def kernel(
    rate_z, rate_w,
    x_hbm, z_hbm, w_hbm, mask, modality_hbm, z_out, w_out,
    x, obs, zb, zt, zf, wf, wg, own, sib_out, sib_in, ring_out, ring_in, x_out, x_in, pair_out, pair_in,
    g_local, g_sib, g_half, g_pair, g_z, g_all, pz, z_in_parts, z_new,
    z_in, w_in, w_new, modality, x_sem, in_sem, out_sem, ag_s, ag_r, agx_s, agx_r, ags_s, ags_r, rs_s, rs_r, rsa_s, rsa_r, rsx_s, rsx_r, rss_s, rss_r,
    g_s, g_r, gz_s, gz_r, gf_s, gf_r, az_s, az_r, an_s, an_r,
):
    s = lax.axis_index("sample")
    k = lax.axis_index("feat")
    z = s // 4
    xh = (s // 2) % 2
    c = s % 2
    batch = z // 4
    sibling = {"sample": z * 4 + xh * 2 + (1 - c)}
    partner = {"sample": z * 4 + (1 - xh) * 2 + c}

    def along(step):
        return {"sample": ((z + step + NZ) % NZ) * 4 + xh * 2 + c}

    def peer(off):
        return {"feat": (k + off) % NF}

    neighbour = (along(1), along(-1))
    started = []

    def copy(src, dst, send, recv, device):
        return pltpu.make_async_remote_copy(
            src_ref=src, dst_ref=dst, send_sem=send, recv_sem=recv,
            device_id=device, device_id_type=pl.DeviceIdType.MESH,
        )

    def send(*args):
        one = copy(*args)
        one.start()
        started.append(one)

    def shard(rel_z, col, core):
        which = xh if col == 0 else 1 - xh
        return ((z + rel_z + NZ) % NZ) * 4 + which * 2 + core

    load_x = pltpu.make_async_copy(x_hbm, x, x_sem)
    loads = [
        pltpu.make_async_copy(there, here, in_sem.at[i])
        for i, (there, here) in enumerate(((w_hbm, w_in), (z_hbm, z_in), (modality_hbm, modality)))
    ]
    for one in loads:
        one.start()
    load_x.start()

    barrier = pltpu.get_barrier_semaphore()
    greet = [sibling, partner] + [along(d) for d in range(1, NZ)] + [peer(d) for d in range(1, NF)]
    for device in greet:
        pl.semaphore_signal(barrier, inc=1, device_id=device, device_id_type=pl.DeviceIdType.MESH)
    loads[0].wait()
    wg[0, s] = w_in[...].astype(BF)
    loads[1].wait()
    zb[0] = z_in[...].astype(BF)
    loads[2].wait()
    pl.semaphore_wait(barrier, len(greet))

    waited = set()

    def once(key, copies):
        if key not in waited:
            waited.add(key)
            copies().wait_recv()

    def rows(h):
        return pl.ds(h * H, H)

    def ag_send(it, d, kind, t):
        col, h = KINDS[kind]
        block = wg.at[it, shard(-t if d == 0 else t, col, c), rows(h)]
        i = ((it * 2 + d) * 3 + kind) * 4 + t
        send(block, block, ag_s.at[i], ag_r.at[i], neighbour[d])

    def ag_sibling(it, rel, col, h):
        block = wg.at[it, shard(rel, col, c), rows(h)]
        i = ((it * NZ + rel % NZ) * 2 + col) * 2 + h
        send(block, block, ags_s.at[i], ags_r.at[i], sibling)

    def ag_across(it, rel, h):
        block = wg.at[it, shard(rel, 0, c), rows(h)]
        i = it * (NZ + 1) + (NZ if h else rel % NZ)
        send(block, block, agx_s.at[i], agx_r.at[i], partner)

    def ag_begin(it):
        for kind in (0, 1):
            for d in (0, 1):
                ag_send(it, d, kind, 0)
        ag_across(it, 0, 1)
        ag_across(it, 0, 0)
        ag_sibling(it, 0, 0, 0)
        ag_sibling(it, 0, 0, 1)

    def ag_pair(it):
        block = wg.at[it, shard(0, 1, c), rows(1)]
        i = it * (NZ + 1) + NZ
        copy(block, block, agx_s.at[i], agx_r.at[i], partner).wait_recv()
        for d in (0, 1):
            ag_send(it, d, 2, 0)
        ag_sibling(it, 0, 1, 1)

    def ag_one(it, d, kind, t):
        col, h = KINDS[kind]
        full = (d, kind) in AG_FULL
        rel = -(t + 1) if d == 0 else t + 1
        block = wg.at[it, shard(rel, col, c), rows(h)]
        i = ((it * 2 + d) * 3 + kind) * 4 + t
        copy(block, block, ag_s.at[i], ag_r.at[i], neighbour[d]).wait_recv()
        if t < 2 or (t == 2 and full):
            ag_send(it, d, kind, t + 1)
        if kind == 0:
            ag_across(it, rel, 0)
        ag_sibling(it, rel, col, h)

    def ag_crossed(it, rel):
        block = wg.at[it, shard(rel, 1, c), rows(0)]
        i = it * (NZ + 1) + rel % NZ
        copy(block, block, agx_s.at[i], agx_r.at[i], partner).wait_recv()
        ag_sibling(it, rel, 1, 0)

    def ag_from_sibling(it, rel):
        for col, h in ((0, 0), (0, 1), (1, 1), (1, 0)):
            block = wg.at[it, shard(rel, col, 1 - c), rows(h)]
            i = ((it * NZ + rel % NZ) * 2 + col) * 2 + h
            copy(block, block, ags_s.at[i], ags_r.at[i], sibling).wait_recv()

    def factor_part(it, rel):
        ag_from_sibling(it, rel)
        first = ("pz", it) not in waited
        waited.add(("pz", it))
        there = (z + rel + NZ) % NZ

        def body(j, carry):
            w = wg[it, pl.ds(there * 4 + j * 2, 2)].reshape(2 * T, T)
            cols = pl.ds(pl.multiple_of(there * 4 * T + j * 2 * T, 2 * T), 2 * T)
            pred = nt(zb[it], w)
            resid = (obs[batch, :, cols] * (pred - x[:, cols].astype(F32))).astype(BF)
            pz[it] += nn(resid, w)
            return carry

        if first:
            pz[it] = jnp.zeros((T, T), F32)
        lax.fori_loop(0, 2, body, 0)

    def cross(it, rel):
        there = (z + rel) % NZ

        def body(col, carry):
            which = (xh + col) % 2
            slot = rel * 2 + col
            for mine in (False, True):
                core = c if mine else 1 - c
                cols = pl.ds(pl.multiple_of((there * 4 + which * 2 + core) * T, T), T)
                value = nn(zt[...], x[:, cols]) * obs[batch, :, cols]
                if mine:
                    own[slot] = value
                else:
                    sib_out[it, slot] = value.astype(BF)
                    sem = it * 2 * NZ + slot
                    copy(
                        sib_out.at[it, slot], sib_in.at[it, slot], rss_s.at[sem], rss_r.at[sem], sibling
                    ).start()
            return carry

        lax.fori_loop(0, 2, body, 0)

    def cross_end(it):
        def body(slot, carry):
            sem = it * 2 * NZ + slot
            copy(
                sib_out.at[it, slot], sib_in.at[it, slot], rss_s.at[sem], rss_r.at[sem], sibling
            ).wait_send()
            return carry

        lax.fori_loop(0, 2 * NZ, body, 0)

    def chip_sum(it, rel, col, h):
        slot = (rel % NZ) * 2 + col
        sem = it * 2 * NZ + slot
        once(("sib", it, slot), lambda: copy(
            sib_out.at[it, slot], sib_in.at[it, slot], rss_s.at[sem], rss_r.at[sem], sibling
        ))
        value = own[slot, rows(h)] + sib_in[it, slot, rows(h)].astype(F32)
        if col == 0 and h == 0:
            i = it * NZ + rel % NZ
            once(("x", it, rel % NZ), lambda: copy(
                x_out.at[i], x_in.at[i], rsa_s.at[i], rsa_r.at[i], partner
            ))
            value = value + x_in[i].astype(F32)
        return value

    def rs_across(it, rel):
        i = it * NZ + rel
        x_out[i] = chip_sum(it, rel, 1, 0).astype(BF)
        send(x_out.at[i], x_in.at[i], rsa_s.at[i], rsa_r.at[i], partner)

    def arrived(it, d, kind, t):
        i = ((it * 2 + d) * 3 + kind) * 4 + t
        copy(ring_out.at[i], ring_in.at[i], rs_s.at[i], rs_r.at[i], neighbour[d]).wait_recv()
        return ring_in[i].astype(F32)

    def rs_one(it, d, kind, t):
        col, h = KINDS[kind]
        value = chip_sum(it, 4 - t if d == 0 else t - 4, col, h)
        if t > 1 or (t == 1 and (d, kind) in RS_FULL):
            value = value + arrived(it, d, kind, t - 1)
        i = ((it * 2 + d) * 3 + kind) * 4 + t
        ring_out[i] = value.astype(BF)
        send(ring_out.at[i], ring_in.at[i], rs_s.at[i], rs_r.at[i], neighbour[d])

    def rs_pair_send(it):
        value = chip_sum(it, 0, 1, 1) + arrived(it, 0, 2, 3) + arrived(it, 1, 2, 3)
        pair_out[it] = value.astype(BF)
        send(pair_out.at[it], pair_in.at[it], rsx_s.at[it], rsx_r.at[it], partner)

    def rs_end(it):
        low = chip_sum(it, 0, 0, 0) + arrived(it, 0, 0, 3) + arrived(it, 1, 0, 3)
        high = chip_sum(it, 0, 0, 1) + arrived(it, 0, 1, 3) + arrived(it, 1, 1, 3)
        copy(pair_out.at[it], pair_in.at[it], rsx_s.at[it], rsx_r.at[it], partner).wait_recv()
        return jnp.concatenate([low, high + pair_in[it].astype(F32)], axis=0)

    half = pl.multiple_of(k * 32 + c * 16, 16)
    other_half = pl.multiple_of(k * 32 + (1 - c) * 16, 16)
    base = pl.multiple_of(k * 32 + c * 16 + xh * 8, 8)
    mine8 = pl.multiple_of(xh * 8, 8)
    other8 = pl.multiple_of((1 - xh) * 8, 8)

    def gram(it):
        zt[...] = zb[it].astype(F32).T.astype(BF)
        g_local[it] = nn(zt[...], zb[it])
        i = it * 4
        send(g_local.at[it, pl.ds(other_half, 16)], g_sib.at[it], g_s.at[i], g_r.at[i], sibling)

    def gram_pair(it):
        i = it * 4
        copy(g_half.at[it], g_sib.at[it], g_s.at[i], g_r.at[i], sibling).wait_recv()
        g_half[it] = g_local[it, pl.ds(half, 16)] + g_sib[it]
        i = it * 4 + 1
        send(g_half.at[it, pl.ds(other8, 8)], g_pair.at[it], g_s.at[i], g_r.at[i], partner)

    def gram_z(it):
        i = it * 4 + 1
        copy(g_pair.at[it], g_pair.at[it], g_s.at[i], g_r.at[i], partner).wait_recv()
        g_z[it, z] = g_half[it, pl.ds(mine8, 8)] + g_pair[it]
        for off in range(1, NZ):
            i = it * NZ + off
            send(g_z.at[it, z], g_z.at[it, z], gz_s.at[i], gz_r.at[i], along(off))

    def gram_batches(it):
        for off in range(1, NZ):
            i = it * NZ + off
            slot = g_z.at[it, (z + NZ - off) % NZ]
            copy(slot, slot, gz_s.at[i], gz_r.at[i], along(off)).wait_recv()
        for b in (0, 1):
            g_all[it, b, pl.ds(base, 8)] = (
                (g_z[it, 4 * b] + g_z[it, 4 * b + 1]) + (g_z[it, 4 * b + 2] + g_z[it, 4 * b + 3])
            )
        block = g_all.at[it, :, pl.ds(base, 8)]
        send(block, block, g_s.at[it * 4 + 2], g_r.at[it * 4 + 2], partner)

    def gram_sibling(it):
        rows = pl.multiple_of(k * 32 + c * 16 + (1 - xh) * 8, 8)
        block = g_all.at[it, :, pl.ds(rows, 8)]
        copy(block, block, g_s.at[it * 4 + 2], g_r.at[it * 4 + 2], partner).wait_recv()
        block = g_all.at[it, :, pl.ds(half, 16)]
        send(block, block, g_s.at[it * 4 + 3], g_r.at[it * 4 + 3], sibling)

    def gram_feat(it):
        block = g_all.at[it, :, pl.ds(other_half, 16)]
        copy(block, block, g_s.at[it * 4 + 3], g_r.at[it * 4 + 3], sibling).wait_recv()
        block = g_all.at[it, :, pl.ds(pl.multiple_of(k * 32, 32), 32)]
        for off in range(1, NF):
            i = it * NF + off
            send(block, block, gf_s.at[i], gf_r.at[i], peer(off))

    def new_loadings(it):
        for off in range(1, NF):
            i = it * NF + off
            rows = pl.multiple_of(((k + NF - off) % NF) * 32, 32)
            block = g_all.at[it, :, pl.ds(rows, 32)]
            copy(block, block, gf_s.at[i], gf_r.at[i], peer(off)).wait_recv()
        cols = pl.ds(pl.multiple_of(s * T, T), T)
        w = wg[it, s]
        grad = jnp.zeros((T, T), F32)
        for b in (0, 1):
            g = g_all[it, b]
            high = g.astype(BF)
            low = (g - high.astype(F32)).astype(BF)
            grad = grad + obs[b, :, cols] * (nt(high, w) + nt(low, w))
        grad = grad - rs_end(it)
        new = (w_in[...] if it == 0 else wf[...]) - rate_w * grad.T
        if it == 0:
            wf[...] = new
            wg[1, s] = new.astype(BF)
        else:
            w_new[...] = new
            pltpu.make_async_copy(w_new, w_out, out_sem.at[0]).start()

    rows32 = pl.multiple_of(k * 32, 32)

    def factors_send(it):
        for off in range(1, NF):
            i = it * NF + off
            rows = pl.multiple_of(((k + off) % NF) * 32, 32)
            send(pz.at[it, pl.ds(rows, 32)], z_in_parts.at[it, off], az_s.at[i], az_r.at[i], peer(off))

    def factors_sum(it):
        total = pz[it, pl.ds(rows32, 32)]
        for off in range(1, NF):
            i = it * NF + off
            slot = z_in_parts.at[it, off]
            copy(slot, slot, az_s.at[i], az_r.at[i], peer(off)).wait_recv()
            total = total + z_in_parts[it, off]
        old = z_in[pl.ds(rows32, 32)] if it == 0 else zf[...]
        new = old - rate_z * total
        if it == 0:
            zf[...] = new
            zb[1, pl.ds(rows32, 32)] = new.astype(BF)
        else:
            z_new[pl.ds(rows32, 32)] = new
        target = zb.at[1] if it == 0 else z_new
        block = target.at[pl.ds(rows32, 32)]
        for off in range(1, NF):
            i = it * NF + off
            send(block, block, an_s.at[i], an_r.at[i], peer(off))

    def factors_wait(it):
        target = zb.at[1] if it == 0 else z_new
        for off in range(1, NF):
            i = it * NF + off
            block = target.at[pl.ds(pl.multiple_of(((k + NF - off) % NF) * 32, 32), 32)]
            copy(block, block, an_s.at[i], an_r.at[i], peer(off)).wait_recv()
        if it == 1:
            pltpu.make_async_copy(z_new, z_out, out_sem.at[1]).start()

    def load():
        for b in (0, 1):
            seen = jnp.zeros(modality.shape, F32)
            for m in range(MODS):
                seen = jnp.where(modality[...] == m, mask[b, m].astype(F32), seen)
            obs[b] = seen
        load_x.wait()

    do = {
        "agb": ag_begin, "agp": ag_pair, "ag": ag_one, "agc": ag_crossed, "fp": factor_part,
        "fs": factors_send, "fsum": factors_sum, "fw": factors_wait,
        "gram": gram, "gp": gram_pair, "gz": gram_z, "gb": gram_batches, "gs": gram_sibling, "gf": gram_feat,
        "cr": cross, "rx": rs_across, "rs": rs_one, "rp": rs_pair_send, "nl": new_loadings, "ld": load,
    }
    for name, *where in ORDER:
        do[name](*where)

    for one in started:
        one.wait_send()
    for it in range(ITERS):
        cross_end(it)
    pltpu.make_async_copy(w_new, w_out, out_sem.at[0]).wait()
    pltpu.make_async_copy(z_new, z_out, out_sem.at[1]).wait()


def hand_over(z_from, w_from, z_to, w_to):
    z_to[...] = z_from[...]
    w_to[...] = w_from[...]


def per_device(expression, factors, loadings, batch_mask, modality):
    rows = factors.shape[0]
    rank = factors.shape[1]
    cells = rows * lax.axis_size("sample")
    width = expression.shape[1]
    features = width * lax.axis_size("feat")
    rate_z = 0.9 * math.sqrt(rank) / features
    rate_w = 0.9 * math.sqrt(rank) / cells
    hbm = pl.BlockSpec(memory_space=pl.ANY)
    vm = pl.BlockSpec(memory_space=pltpu.VMEM)
    dma = lambda n: pltpu.SemaphoreType.DMA((n,))
    out = jax.ShapeDtypeStruct((T, T), F32)

    def body(*refs):
        kernel(rate_z, rate_w, *refs)

    z_out, w_out = pl.pallas_call(
        body,
        out_shape=(out, out),
        in_specs=[
            hbm, hbm, hbm, pl.BlockSpec(memory_space=pltpu.SMEM), hbm,
        ],
        out_specs=(hbm, hbm),
        scratch_shapes=[
            pltpu.VMEM((rows, width), BF),
            pltpu.VMEM((2, 1, width), F32),
            pltpu.VMEM((ITERS, T, T), BF),
            pltpu.VMEM((T, T), BF),
            pltpu.VMEM((32, T), F32),
            pltpu.VMEM((T, T), F32),
            pltpu.VMEM((ITERS, 32, T, T), BF),
            pltpu.VMEM((2 * NZ, T, T), F32),
            pltpu.VMEM((ITERS, 2 * NZ, T, T), BF),
            pltpu.VMEM((ITERS, 2 * NZ, T, T), BF),
            pltpu.VMEM((ITERS * 24, H, T), BF),
            pltpu.VMEM((ITERS * 24, H, T), BF),
            pltpu.VMEM((ITERS * NZ, H, T), BF),
            pltpu.VMEM((ITERS * NZ, H, T), BF),
            pltpu.VMEM((ITERS, H, T), BF),
            pltpu.VMEM((ITERS, H, T), BF),
            pltpu.VMEM((ITERS, T, T), F32),
            pltpu.VMEM((ITERS, 16, T), F32),
            pltpu.VMEM((ITERS, 16, T), F32),
            pltpu.VMEM((ITERS, 8, T), F32),
            pltpu.VMEM((ITERS, NZ, 8, T), F32),
            pltpu.VMEM((ITERS, 2, T, T), F32),
            pltpu.VMEM((ITERS, T, T), F32),
            pltpu.VMEM((ITERS, NF, 32, T), F32),
            pltpu.VMEM((T, T), F32),
            pltpu.VMEM((T, T), F32),
            pltpu.VMEM((T, T), F32),
            pltpu.VMEM((T, T), F32),
            pltpu.VMEM((1, width), jnp.int32),
            pltpu.SemaphoreType.DMA,
            dma(3), dma(2),
            dma(ITERS * 24), dma(ITERS * 24),
            dma(ITERS * (NZ + 1)), dma(ITERS * (NZ + 1)),
            dma(ITERS * 32), dma(ITERS * 32),
            dma(ITERS * 24), dma(ITERS * 24),
            dma(ITERS * NZ), dma(ITERS * NZ),
            dma(ITERS), dma(ITERS),
            dma(ITERS * 16), dma(ITERS * 16),
            dma(ITERS * 4), dma(ITERS * 4),
            dma(ITERS * NZ), dma(ITERS * NZ),
            dma(ITERS * NF), dma(ITERS * NF),
            dma(ITERS * NF), dma(ITERS * NF),
            dma(ITERS * NF), dma(ITERS * NF),
        ],
        compiler_params=pltpu.CompilerParams(
            collective_id=0, has_side_effects=True, vmem_limit_bytes=60 * 1024 * 1024
        ),
    )(expression, factors, loadings, batch_mask, modality.reshape(1, width))
    return pl.pallas_call(
        hand_over,
        out_shape=(out, out),
        in_specs=[vm, vm],
        out_specs=(vm, vm),
    )(z_out, w_out)


def solution(mesh):
    return jax.shard_map(
        per_device,
        mesh=mesh,
        in_specs=(
            P("sample", "feat"),
            P("sample", None),
            P(("feat", "sample"), None),
            P(),
            P("feat"),
        ),
        out_specs=(P("sample", None), P(("feat", "sample"), None)),
        check_vma=False,
    )
```

```python
import math

import jax
import jax.numpy as jnp
from jax import lax
from jax.experimental import pallas as pl
from jax.experimental.pallas import tpu as pltpu
from jax.sharding import PartitionSpec as P

ITERS = 2
NZ = 8
T = 256
MODS = 5
BF = jnp.bfloat16
F32 = jnp.float32
H = T // 2
KINDS = ((0, 0), (0, 1), (1, 1))
AG_FULL = ((0, 0), (0, 1), (1, 2))
RS_FULL = ((1, 0), (1, 1), (0, 2))
ORDER = (
    ("ld",), ("gram", 0), ("cr", 0, 4), ("cr", 0, 3), ("cr", 0, 5), ("cr", 0, 2), ("cr", 0, 6), ("cr", 0, 1),
    ("cr", 0, 7), ("cr", 0, 0), ("bar",), ("agb", 0), ("gms", 0), ("crs", 4), ("crs", 5), ("crs", 2),
    ("crs", 1), ("crs", 3), ("crs", 6), ("crs", 0), ("crs", 7), ("gp", 0), ("rs", 0, 1, 1, 0), ("rx", 0, 4),
    ("rs", 0, 0, 2, 0), ("agp", 0), ("rx", 0, 5), ("rs", 0, 1, 2, 1), ("ag", 0, 0, 0, 0), ("ag", 0, 1, 0, 0),
    ("agc", 0, 0), ("gz", 0), ("rx", 0, 2), ("ag", 0, 0, 1, 0), ("ag", 0, 1, 1, 0), ("rx", 0, 1),
    ("rs", 0, 1, 0, 0), ("rs", 0, 0, 1, 1), ("rx", 0, 3), ("rs", 0, 0, 2, 1), ("rs", 0, 1, 1, 1), ("rx", 0, 6),
    ("ag", 0, 1, 2, 0), ("ag", 0, 0, 2, 0), ("agc", 0, 7), ("rx", 0, 0), ("rs", 0, 1, 2, 2),
    ("ag", 0, 0, 0, 1), ("rx", 0, 7), ("agc", 0, 1), ("ag", 0, 1, 0, 1), ("fp", 0, 0), ("fp", 0, 7),
    ("fp", 0, 1), ("rs", 0, 0, 1, 2), ("rs", 0, 0, 0, 1), ("gb", 0), ("ag", 0, 0, 1, 1), ("ag", 0, 1, 1, 1),
    ("rs", 0, 1, 0, 1), ("rs", 0, 0, 2, 2), ("rs", 0, 1, 1, 2), ("ag", 0, 0, 2, 1), ("ag", 0, 1, 2, 1),
    ("ag", 0, 0, 0, 2), ("agc", 0, 6), ("rs", 0, 1, 2, 3), ("rs", 0, 0, 1, 3), ("fp", 0, 6),
    ("ag", 0, 1, 0, 2), ("rs", 0, 0, 0, 2), ("agc", 0, 2), ("gs", 0), ("ag", 0, 1, 1, 2), ("ag", 0, 0, 1, 2),
    ("fp", 0, 2), ("gf", 0), ("agc", 0, 5), ("rs", 0, 1, 0, 2), ("rs", 0, 0, 2, 3), ("agc", 0, 3),
    ("rs", 0, 1, 1, 3), ("ag", 0, 0, 2, 2), ("ag", 0, 1, 2, 2), ("ag", 0, 0, 0, 3), ("gy", 0), ("fp", 0, 5),
    ("fp", 0, 3), ("rs", 0, 1, 0, 3), ("rs", 0, 0, 0, 3), ("agc", 0, 4), ("ag", 0, 0, 1, 3),
    ("ag", 0, 1, 2, 3), ("rp", 0), ("fp", 0, 4), ("fs", 0), ("nl", 0), ("agb", 1), ("fx", 0), ("agp", 1),
    ("ag", 1, 0, 0, 0), ("ag", 1, 1, 0, 0), ("agc", 1, 0), ("ag", 1, 0, 1, 0), ("ag", 1, 1, 1, 0), ("fsum", 0),
    ("ag", 1, 0, 2, 0), ("ag", 1, 1, 2, 0), ("agc", 1, 7), ("ag", 1, 0, 0, 1), ("ag", 1, 1, 0, 1), ("fw", 0),
    ("gram", 1), ("gms", 1), ("cr", 1, 4), ("agc", 1, 1), ("cr", 1, 3), ("ag", 1, 1, 1, 1), ("ag", 1, 0, 1, 1),
    ("gp", 1), ("cr", 1, 5), ("cr", 1, 2), ("ag", 1, 0, 2, 1), ("rx", 1, 4), ("agc", 1, 6), ("ag", 1, 1, 2, 1),
    ("cr", 1, 6), ("cr", 1, 1), ("ag", 1, 0, 0, 2), ("ag", 1, 1, 0, 2), ("rx", 1, 3), ("cr", 1, 7),
    ("cr", 1, 0), ("gz", 1), ("ag", 1, 0, 1, 2), ("ag", 1, 1, 1, 2), ("agc", 1, 2), ("rx", 1, 5), ("fp", 1, 0),
    ("ag", 1, 0, 2, 2), ("ag", 1, 1, 2, 2), ("rx", 1, 2), ("agc", 1, 5), ("rs", 1, 0, 2, 0), ("fp", 1, 7),
    ("ag", 1, 0, 0, 3), ("agc", 1, 3), ("rx", 1, 6), ("rs", 1, 1, 0, 0), ("rs", 1, 0, 1, 1), ("fp", 1, 1),
    ("gb", 1), ("rx", 1, 1), ("rs", 1, 0, 0, 1), ("rs", 1, 1, 2, 1), ("rs", 1, 1, 1, 0), ("fp", 1, 6),
    ("ag", 1, 0, 1, 3), ("ag", 1, 1, 2, 3), ("rx", 1, 7), ("rx", 1, 0), ("rs", 1, 0, 2, 1), ("fp", 1, 2),
    ("rs", 1, 1, 0, 1), ("fp", 1, 5), ("agc", 1, 4), ("rs", 1, 1, 2, 2), ("rs", 1, 0, 1, 2), ("fp", 1, 3),
    ("rs", 1, 0, 0, 2), ("gs", 1), ("rs", 1, 1, 1, 1), ("fp", 1, 4), ("fs", 1), ("gf", 1), ("rs", 1, 0, 2, 2),
    ("rs", 1, 1, 0, 2), ("rs", 1, 0, 1, 3), ("rs", 1, 1, 2, 3), ("rs", 1, 0, 0, 3), ("rs", 1, 1, 1, 2),
    ("gy", 1), ("fx", 1), ("rs", 1, 0, 2, 3), ("rs", 1, 1, 0, 3), ("fsum", 1), ("rs", 1, 1, 1, 3), ("rp", 1),
    ("nl", 1), ("fw", 1),
)


def nn(a, b):
    return jnp.dot(a, b, preferred_element_type=F32)


def nt(a, b):
    return lax.dot_general(a, b, (((1,), (1,)), ((), ())), preferred_element_type=F32)


def kernel(
    rate_z, rate_w,
    x_hbm, z_hbm, w_hbm, mask, modality_hbm, z_out, w_out,
    x, obs, zb, zt, zf, wf, wg, own, sib_out, sib_in, ring_out, ring_in, x_out, x_in, pair_out, pair_in,
    g_local, g_sib, g_half, g_pair, g_z, g_all, pz, z_in_parts, z_sum, z_new,
    z_in, w_in, w_new, modality, x_sem, in_sem, out_sem, ag_s, ag_r, agx_s, agx_r, ags_s, ags_r, rs_s, rs_r, rsa_s, rsa_r, rsx_s, rsx_r, rss_s, rss_r,
    g_s, g_r, gz_s, gz_r, gf_s, gf_r, az_s, az_r, an_s, an_r,
):
    s = lax.axis_index("sample")
    k = lax.axis_index("feat")
    z = s // 4
    xh = (s // 2) % 2
    c = s % 2
    batch = z // 4
    xl = k // 4
    y = k % 4
    sibling = {"sample": z * 4 + xh * 2 + (1 - c)}
    partner = {"sample": z * 4 + (1 - xh) * 2 + c}

    def along(step):
        return {"sample": ((z + step + NZ) % NZ) * 4 + xh * 2 + c}

    def y_peer(off):
        return {"feat": xl * 4 + (y + off) % 4}

    x_peer = {"feat": (1 - xl) * 4 + y}

    neighbour = (along(1), along(-1))
    started = []

    def copy(src, dst, send, recv, device):
        return pltpu.make_async_remote_copy(
            src_ref=src, dst_ref=dst, send_sem=send, recv_sem=recv,
            device_id=device, device_id_type=pl.DeviceIdType.MESH,
        )

    def send(*args):
        one = copy(*args)
        one.start()
        started.append(one)

    def shard(rel_z, col, core):
        which = xh if col == 0 else 1 - xh
        return ((z + rel_z + NZ) % NZ) * 4 + which * 2 + core

    load_x = pltpu.make_async_copy(x_hbm, x, x_sem)
    loads = [
        pltpu.make_async_copy(there, here, in_sem.at[i])
        for i, (there, here) in enumerate(((w_hbm, w_in), (z_hbm, z_in), (modality_hbm, modality)))
    ]
    for one in loads:
        one.start()
    load_x.start()

    barrier = pltpu.get_barrier_semaphore()
    greet = [sibling, partner] + [along(d) for d in range(1, NZ)] + [y_peer(d) for d in (1, 2, 3)] + [x_peer]
    for device in greet:
        pl.semaphore_signal(barrier, inc=1, device_id=device, device_id_type=pl.DeviceIdType.MESH)
    loads[0].wait()
    wg[0, s] = w_in[...].astype(BF)
    loads[1].wait()
    zb[0] = z_in[...].astype(BF)
    loads[2].wait()

    waited = set()

    def once(key, copies):
        if key not in waited:
            waited.add(key)
            copies().wait_recv()

    def rows(h):
        return pl.ds(h * H, H)

    def ag_send(it, d, kind, t):
        col, h = KINDS[kind]
        block = wg.at[it, shard(-t if d == 0 else t, col, c), rows(h)]
        i = ((it * 2 + d) * 3 + kind) * 4 + t
        send(block, block, ag_s.at[i], ag_r.at[i], neighbour[d])

    def ag_sibling(it, rel, col, h):
        block = wg.at[it, shard(rel, col, c), rows(h)]
        i = ((it * NZ + rel % NZ) * 2 + col) * 2 + h
        send(block, block, ags_s.at[i], ags_r.at[i], sibling)

    def ag_across(it, rel, h):
        block = wg.at[it, shard(rel, 0, c), rows(h)]
        i = it * (NZ + 1) + (NZ if h else rel % NZ)
        send(block, block, agx_s.at[i], agx_r.at[i], partner)

    def ag_begin(it):
        for kind in (0, 1):
            for d in (0, 1):
                ag_send(it, d, kind, 0)
        ag_across(it, 0, 1)
        ag_across(it, 0, 0)
        ag_sibling(it, 0, 0, 0)
        ag_sibling(it, 0, 0, 1)

    def ag_pair(it):
        block = wg.at[it, shard(0, 1, c), rows(1)]
        i = it * (NZ + 1) + NZ
        copy(block, block, agx_s.at[i], agx_r.at[i], partner).wait_recv()
        for d in (0, 1):
            ag_send(it, d, 2, 0)
        ag_sibling(it, 0, 1, 1)

    def ag_one(it, d, kind, t):
        col, h = KINDS[kind]
        full = (d, kind) in AG_FULL
        rel = -(t + 1) if d == 0 else t + 1
        block = wg.at[it, shard(rel, col, c), rows(h)]
        i = ((it * 2 + d) * 3 + kind) * 4 + t
        copy(block, block, ag_s.at[i], ag_r.at[i], neighbour[d]).wait_recv()
        if t < 2 or (t == 2 and full):
            ag_send(it, d, kind, t + 1)
        if kind == 0:
            ag_across(it, rel, 0)
        ag_sibling(it, rel, col, h)

    def ag_crossed(it, rel):
        block = wg.at[it, shard(rel, 1, c), rows(0)]
        i = it * (NZ + 1) + rel % NZ
        copy(block, block, agx_s.at[i], agx_r.at[i], partner).wait_recv()
        ag_sibling(it, rel, 1, 0)

    def ag_from_sibling(it, rel):
        for col, h in ((0, 0), (0, 1), (1, 1), (1, 0)):
            block = wg.at[it, shard(rel, col, 1 - c), rows(h)]
            i = ((it * NZ + rel % NZ) * 2 + col) * 2 + h
            copy(block, block, ags_s.at[i], ags_r.at[i], sibling).wait_recv()

    def factor_part(it, rel):
        ag_from_sibling(it, rel)
        first = ("pz", it) not in waited
        waited.add(("pz", it))
        there = (z + rel + NZ) % NZ

        def body(j, carry):
            w = wg[it, pl.ds(there * 4 + j * 2, 2)].reshape(2 * T, T)
            cols = pl.ds(pl.multiple_of(there * 4 * T + j * 2 * T, 2 * T), 2 * T)
            pred = nt(zb[it], w)
            resid = (obs[batch, :, cols] * (pred - x[:, cols].astype(F32))).astype(BF)
            pz[it] += nn(resid, w)
            return carry

        if first:
            pz[it] = jnp.zeros((T, T), F32)
        lax.fori_loop(0, 2, body, 0)

    def cross(it, rel):
        there = (z + rel) % NZ

        def body(col, carry):
            which = (xh + col) % 2
            slot = rel * 2 + col
            for mine in (False, True):
                core = c if mine else 1 - c
                cols = pl.ds(pl.multiple_of((there * 4 + which * 2 + core) * T, T), T)
                value = nn(zt[...], x[:, cols]) * obs[batch, :, cols]
                if mine:
                    own[slot] = value
                else:
                    sib_out[it, slot] = value.astype(BF)
                    if it == 1:
                        sem = it * 2 * NZ + slot
                        copy(
                            sib_out.at[it, slot], sib_in.at[it, slot], rss_s.at[sem], rss_r.at[sem], sibling
                        ).start()
            return carry

        lax.fori_loop(0, 2, body, 0)

    def cross_send(rel):
        for col in (0, 1):
            slot = rel * 2 + col
            copy(
                sib_out.at[0, slot], sib_in.at[0, slot], rss_s.at[slot], rss_r.at[slot], sibling
            ).start()

    def cross_end(it):
        def body(slot, carry):
            sem = it * 2 * NZ + slot
            copy(
                sib_out.at[it, slot], sib_in.at[it, slot], rss_s.at[sem], rss_r.at[sem], sibling
            ).wait_send()
            return carry

        lax.fori_loop(0, 2 * NZ, body, 0)

    def chip_sum(it, rel, col, h):
        slot = (rel % NZ) * 2 + col
        sem = it * 2 * NZ + slot
        once(("sib", it, slot), lambda: copy(
            sib_out.at[it, slot], sib_in.at[it, slot], rss_s.at[sem], rss_r.at[sem], sibling
        ))
        value = own[slot, rows(h)] + sib_in[it, slot, rows(h)].astype(F32)
        if col == 0 and h == 0:
            i = it * NZ + rel % NZ
            once(("x", it, rel % NZ), lambda: copy(
                x_out.at[i], x_in.at[i], rsa_s.at[i], rsa_r.at[i], partner
            ))
            value = value + x_in[i].astype(F32)
        return value

    def rs_across(it, rel):
        i = it * NZ + rel
        x_out[i] = chip_sum(it, rel, 1, 0).astype(BF)
        send(x_out.at[i], x_in.at[i], rsa_s.at[i], rsa_r.at[i], partner)

    def arrived(it, d, kind, t):
        i = ((it * 2 + d) * 3 + kind) * 4 + t
        copy(ring_out.at[i], ring_in.at[i], rs_s.at[i], rs_r.at[i], neighbour[d]).wait_recv()
        return ring_in[i].astype(F32)

    def rs_one(it, d, kind, t):
        col, h = KINDS[kind]
        value = chip_sum(it, 4 - t if d == 0 else t - 4, col, h)
        if t > 1 or (t == 1 and (d, kind) in RS_FULL):
            value = value + arrived(it, d, kind, t - 1)
        i = ((it * 2 + d) * 3 + kind) * 4 + t
        ring_out[i] = value.astype(BF)
        send(ring_out.at[i], ring_in.at[i], rs_s.at[i], rs_r.at[i], neighbour[d])

    def rs_pair_send(it):
        value = chip_sum(it, 0, 1, 1) + arrived(it, 0, 2, 3) + arrived(it, 1, 2, 3)
        pair_out[it] = value.astype(BF)
        send(pair_out.at[it], pair_in.at[it], rsx_s.at[it], rsx_r.at[it], partner)

    def rs_end(it):
        low = chip_sum(it, 0, 0, 0) + arrived(it, 0, 0, 3) + arrived(it, 1, 0, 3)
        high = chip_sum(it, 0, 0, 1) + arrived(it, 0, 1, 3) + arrived(it, 1, 1, 3)
        copy(pair_out.at[it], pair_in.at[it], rsx_s.at[it], rsx_r.at[it], partner).wait_recv()
        return jnp.concatenate([low, high + pair_in[it].astype(F32)], axis=0)

    rows64 = pl.multiple_of(y * 64, 64)

    kk = y * 2 + xl
    half = pl.multiple_of(kk * 32 + c * 16, 16)
    other_half = pl.multiple_of(kk * 32 + (1 - c) * 16, 16)
    base = pl.multiple_of(kk * 32 + c * 16 + xh * 8, 8)
    mine8 = pl.multiple_of(xh * 8, 8)
    other8 = pl.multiple_of((1 - xh) * 8, 8)

    def gram(it):
        zt[...] = zb[it].astype(F32).T.astype(BF)
        g_local[it] = nn(zt[...], zb[it])

    def gram_send(it):
        i = it * 4
        send(g_local.at[it, pl.ds(other_half, 16)], g_sib.at[it], g_s.at[i], g_r.at[i], sibling)

    def gram_pair(it):
        i = it * 4
        copy(g_half.at[it], g_sib.at[it], g_s.at[i], g_r.at[i], sibling).wait_recv()
        g_half[it] = g_local[it, pl.ds(half, 16)] + g_sib[it]
        i = it * 4 + 1
        send(g_half.at[it, pl.ds(other8, 8)], g_pair.at[it], g_s.at[i], g_r.at[i], partner)

    def gram_z(it):
        i = it * 4 + 1
        copy(g_pair.at[it], g_pair.at[it], g_s.at[i], g_r.at[i], partner).wait_recv()
        g_z[it, z] = g_half[it, pl.ds(mine8, 8)] + g_pair[it]
        for off in range(1, NZ):
            i = it * NZ + off
            send(g_z.at[it, z], g_z.at[it, z], gz_s.at[i], gz_r.at[i], along(off))

    def gram_batches(it):
        for off in range(1, NZ):
            i = it * NZ + off
            slot = g_z.at[it, (z + NZ - off) % NZ]
            copy(slot, slot, gz_s.at[i], gz_r.at[i], along(off)).wait_recv()
        for b in (0, 1):
            g_all[it, b, pl.ds(base, 8)] = (
                (g_z[it, 4 * b] + g_z[it, 4 * b + 1]) + (g_z[it, 4 * b + 2] + g_z[it, 4 * b + 3])
            )
        block = g_all.at[it, :, pl.ds(base, 8)]
        send(block, block, g_s.at[it * 4 + 2], g_r.at[it * 4 + 2], partner)

    def gram_sibling(it):
        rows = pl.multiple_of(kk * 32 + c * 16 + (1 - xh) * 8, 8)
        block = g_all.at[it, :, pl.ds(rows, 8)]
        copy(block, block, g_s.at[it * 4 + 2], g_r.at[it * 4 + 2], partner).wait_recv()
        block = g_all.at[it, :, pl.ds(half, 16)]
        send(block, block, g_s.at[it * 4 + 3], g_r.at[it * 4 + 3], sibling)

    def gram_feat(it):
        block = g_all.at[it, :, pl.ds(other_half, 16)]
        copy(block, block, g_s.at[it * 4 + 3], g_r.at[it * 4 + 3], sibling).wait_recv()
        block = g_all.at[it, :, pl.ds(pl.multiple_of(kk * 32, 32), 32)]
        send(block, block, gf_s.at[it * 4], gf_r.at[it * 4], x_peer)

    def gram_y(it):
        block = g_all.at[it, :, pl.ds(pl.multiple_of(y * 64 + (1 - xl) * 32, 32), 32)]
        copy(block, block, gf_s.at[it * 4], gf_r.at[it * 4], x_peer).wait_recv()
        block = g_all.at[it, :, pl.ds(rows64, 64)]
        for off in (1, 2, 3):
            i = it * 4 + off
            send(block, block, gf_s.at[i], gf_r.at[i], y_peer(off))

    def new_loadings(it):
        for off in (1, 2, 3):
            i = it * 4 + off
            block = g_all.at[it, :, pl.ds(pl.multiple_of(((y + 4 - off) % 4) * 64, 64), 64)]
            copy(block, block, gf_s.at[i], gf_r.at[i], y_peer(off)).wait_recv()
        cols = pl.ds(pl.multiple_of(s * T, T), T)
        w = wg[it, s]
        grad = jnp.zeros((T, T), F32)
        for b in (0, 1):
            g = g_all[it, b]
            high = g.astype(BF)
            low = (g - high.astype(F32)).astype(BF)
            grad = grad + obs[b, :, cols] * (nt(high, w) + nt(low, w))
        grad = grad - rs_end(it)
        new = (w_in[...] if it == 0 else wf[...]) - rate_w * grad.T
        if it == 0:
            wf[...] = new
            wg[1, s] = new.astype(BF)
        else:
            w_new[...] = new
            pltpu.make_async_copy(w_new, w_out, out_sem.at[0]).start()

    def factors_send(it):
        for off in (1, 2, 3):
            i = it * 4 + off
            there = pl.multiple_of(((y + off) % 4) * 64, 64)
            send(pz.at[it, pl.ds(there, 64)], z_in_parts.at[it, off], az_s.at[i], az_r.at[i], y_peer(off))

    def factors_across(it):
        total = pz[it, pl.ds(rows64, 64)]
        for off in (1, 2, 3):
            i = it * 4 + off
            slot = z_in_parts.at[it, off]
            copy(slot, slot, az_s.at[i], az_r.at[i], y_peer(off)).wait_recv()
            total = total + z_in_parts[it, off]
        z_sum[it, 0] = total
        send(z_sum.at[it, 0], z_sum.at[it, 1], az_s.at[it * 4], az_r.at[it * 4], x_peer)

    def factors_sum(it):
        copy(z_sum.at[it, 0], z_sum.at[it, 1], az_s.at[it * 4], az_r.at[it * 4], x_peer).wait_recv()
        old = z_in[pl.ds(rows64, 64)] if it == 0 else zf[...]
        new = old - rate_z * (z_sum[it, 0] + z_sum[it, 1])
        if it == 0:
            zf[...] = new
            zb[1, pl.ds(rows64, 64)] = new.astype(BF)
        else:
            z_new[pl.ds(rows64, 64)] = new
        target = zb.at[1] if it == 0 else z_new
        block = target.at[pl.ds(rows64, 64)]
        for off in (1, 2, 3):
            i = it * 4 + off
            send(block, block, an_s.at[i], an_r.at[i], y_peer(off))

    def factors_wait(it):
        target = zb.at[1] if it == 0 else z_new
        for off in (1, 2, 3):
            i = it * 4 + off
            block = target.at[pl.ds(pl.multiple_of(((y + 4 - off) % 4) * 64, 64), 64)]
            copy(block, block, an_s.at[i], an_r.at[i], y_peer(off)).wait_recv()
        if it == 1:
            pltpu.make_async_copy(z_new, z_out, out_sem.at[1]).start()

    def enter():
        pl.semaphore_wait(barrier, len(greet))

    def load():
        for b in (0, 1):
            seen = jnp.zeros(modality.shape, F32)
            for m in range(MODS):
                seen = jnp.where(modality[...] == m, mask[b, m].astype(F32), seen)
            obs[b] = seen
        load_x.wait()

    do = {
        "agb": ag_begin, "agp": ag_pair, "ag": ag_one, "agc": ag_crossed, "fp": factor_part,
        "fs": factors_send, "fsum": factors_sum, "fw": factors_wait,
        "gram": gram, "gp": gram_pair, "gz": gram_z, "gb": gram_batches, "gs": gram_sibling, "gf": gram_feat,
        "cr": cross, "rx": rs_across, "rs": rs_one, "rp": rs_pair_send, "nl": new_loadings, "ld": load,
        "bar": enter, "crs": cross_send, "gms": gram_send, "gy": gram_y, "fx": factors_across,
    }
    for name, *where in ORDER:
        do[name](*where)

    for one in started:
        one.wait_send()
    for it in range(ITERS):
        cross_end(it)
    pltpu.make_async_copy(w_new, w_out, out_sem.at[0]).wait()
    pltpu.make_async_copy(z_new, z_out, out_sem.at[1]).wait()


def hand_over(z_from, w_from, z_to, w_to):
    z_to[...] = z_from[...]
    w_to[...] = w_from[...]


def per_device(expression, factors, loadings, batch_mask, modality):
    rows = factors.shape[0]
    rank = factors.shape[1]
    cells = rows * lax.axis_size("sample")
    width = expression.shape[1]
    features = width * lax.axis_size("feat")
    rate_z = 0.9 * math.sqrt(rank) / features
    rate_w = 0.9 * math.sqrt(rank) / cells
    hbm = pl.BlockSpec(memory_space=pl.ANY)
    vm = pl.BlockSpec(memory_space=pltpu.VMEM)
    dma = lambda n: pltpu.SemaphoreType.DMA((n,))
    out = jax.ShapeDtypeStruct((T, T), F32)

    def body(*refs):
        kernel(rate_z, rate_w, *refs)

    z_out, w_out = pl.pallas_call(
        body,
        out_shape=(out, out),
        in_specs=[
            hbm, hbm, hbm, pl.BlockSpec(memory_space=pltpu.SMEM), hbm,
        ],
        out_specs=(hbm, hbm),
        scratch_shapes=[
            pltpu.VMEM((rows, width), BF),
            pltpu.VMEM((2, 1, width), F32),
            pltpu.VMEM((ITERS, T, T), BF),
            pltpu.VMEM((T, T), BF),
            pltpu.VMEM((64, T), F32),
            pltpu.VMEM((T, T), F32),
            pltpu.VMEM((ITERS, 32, T, T), BF),
            pltpu.VMEM((2 * NZ, T, T), F32),
            pltpu.VMEM((ITERS, 2 * NZ, T, T), BF),
            pltpu.VMEM((ITERS, 2 * NZ, T, T), BF),
            pltpu.VMEM((ITERS * 24, H, T), BF),
            pltpu.VMEM((ITERS * 24, H, T), BF),
            pltpu.VMEM((ITERS * NZ, H, T), BF),
            pltpu.VMEM((ITERS * NZ, H, T), BF),
            pltpu.VMEM((ITERS, H, T), BF),
            pltpu.VMEM((ITERS, H, T), BF),
            pltpu.VMEM((ITERS, T, T), F32),
            pltpu.VMEM((ITERS, 16, T), F32),
            pltpu.VMEM((ITERS, 16, T), F32),
            pltpu.VMEM((ITERS, 8, T), F32),
            pltpu.VMEM((ITERS, NZ, 8, T), F32),
            pltpu.VMEM((ITERS, 2, T, T), F32),
            pltpu.VMEM((ITERS, T, T), F32),
            pltpu.VMEM((ITERS, 4, 64, T), F32),
            pltpu.VMEM((ITERS, 2, 64, T), F32),
            pltpu.VMEM((T, T), F32),
            pltpu.VMEM((T, T), F32),
            pltpu.VMEM((T, T), F32),
            pltpu.VMEM((T, T), F32),
            pltpu.VMEM((1, width), jnp.int32),
            pltpu.SemaphoreType.DMA,
            dma(3), dma(2),
            dma(ITERS * 24), dma(ITERS * 24),
            dma(ITERS * (NZ + 1)), dma(ITERS * (NZ + 1)),
            dma(ITERS * 32), dma(ITERS * 32),
            dma(ITERS * 24), dma(ITERS * 24),
            dma(ITERS * NZ), dma(ITERS * NZ),
            dma(ITERS), dma(ITERS),
            dma(ITERS * 16), dma(ITERS * 16),
            dma(ITERS * 4), dma(ITERS * 4),
            dma(ITERS * NZ), dma(ITERS * NZ),
            dma(ITERS * 4), dma(ITERS * 4),
            dma(ITERS * 4), dma(ITERS * 4),
            dma(ITERS * 4), dma(ITERS * 4),
        ],
        compiler_params=pltpu.CompilerParams(
            collective_id=0, has_side_effects=True, vmem_limit_bytes=60 * 1024 * 1024
        ),
    )(expression, factors, loadings, batch_mask, modality.reshape(1, width))
    return pl.pallas_call(
        hand_over,
        out_shape=(out, out),
        in_specs=[vm, vm],
        out_specs=(vm, vm),
    )(z_out, w_out)


def solution(mesh):
    return jax.shard_map(
        per_device,
        mesh=mesh,
        in_specs=(
            P("sample", "feat"),
            P("sample", None),
            P(("feat", "sample"), None),
            P(),
            P("feat"),
        ),
        out_specs=(P("sample", None), P(("feat", "sample"), None)),
        check_vma=False,
    )
```

```python
import math

import jax
import jax.numpy as jnp
from jax import lax
from jax.experimental import pallas as pl
from jax.experimental.pallas import tpu as pltpu
from jax.sharding import PartitionSpec as P

ITERS = 2
NZ = 8
T = 256
MODS = 5
BF = jnp.bfloat16
F32 = jnp.float32
H = T // 2
KINDS = ((0, 0), (0, 1), (1, 1))
AG_FULL = ((0, 0), (0, 1), (1, 2))
RS_FULL = ((1, 0), (1, 1), (0, 2))
ORDER = (
    ("ld",), ("gram", 0), ("cr", 0, 4), ("cr", 0, 3), ("cr", 0, 5), ("cr", 0, 2), ("bar",), ("agb", 0),
    ("cr", 0, 6), ("cr", 0, 1), ("cr", 0, 7), ("gms", 0), ("crs", 4), ("cr", 0, 0), ("crs", 5), ("crs", 0),
    ("crs", 3), ("crs", 1), ("crs", 6), ("crs", 7), ("gp", 0), ("crs", 2), ("rs", 0, 1, 1, 0), ("agp", 0),
    ("rx", 0, 4), ("rs", 0, 0, 2, 0), ("ag", 0, 0, 0, 0), ("ag", 0, 1, 0, 0), ("rx", 0, 5), ("gz", 0),
    ("rs", 0, 1, 2, 1), ("agc", 0, 0), ("ag", 0, 0, 1, 0), ("rx", 0, 0), ("ag", 0, 1, 1, 0),
    ("rs", 0, 0, 1, 1), ("rx", 0, 3), ("rs", 0, 1, 0, 0), ("rs", 0, 1, 1, 1), ("ag", 0, 0, 2, 0), ("rx", 0, 1),
    ("agc", 0, 7), ("ag", 0, 1, 2, 0), ("rx", 0, 6), ("rs", 0, 0, 2, 1), ("agc", 0, 1), ("rx", 0, 7),
    ("ag", 0, 1, 0, 1), ("ag", 0, 0, 0, 1), ("rx", 0, 2), ("gb", 0), ("fp", 0, 0), ("fq", 0, 0),
    ("rs", 0, 1, 2, 2), ("fp", 0, 7), ("ag", 0, 0, 1, 1), ("fp", 0, 1), ("rs", 0, 0, 0, 1), ("fq", 0, 1),
    ("rs", 0, 0, 1, 2), ("fq", 0, 7), ("ag", 0, 1, 1, 1), ("rs", 0, 1, 0, 1), ("ag", 0, 0, 2, 1),
    ("rs", 0, 1, 1, 2), ("rs", 0, 0, 2, 2), ("ag", 0, 1, 2, 1), ("ag", 0, 0, 0, 2), ("agc", 0, 2),
    ("ag", 0, 1, 0, 2), ("ag", 0, 0, 1, 2), ("fp", 0, 2), ("agc", 0, 6), ("fq", 0, 2), ("rs", 0, 1, 2, 3),
    ("rs", 0, 0, 0, 2), ("gs", 0), ("fp", 0, 6), ("rs", 0, 0, 1, 3), ("ag", 0, 1, 1, 2), ("fq", 0, 6),
    ("gf", 0), ("agc", 0, 5), ("rs", 0, 1, 0, 2), ("ag", 0, 0, 2, 2), ("agc", 0, 3), ("rs", 0, 1, 1, 3),
    ("fp", 0, 5), ("rs", 0, 0, 2, 3), ("fq", 0, 5), ("ag", 0, 1, 2, 2), ("gy", 0), ("ag", 0, 0, 0, 3),
    ("fp", 0, 3), ("fq", 0, 3), ("ag", 0, 0, 1, 3), ("rs", 0, 1, 0, 3), ("rs", 0, 0, 0, 3), ("agc", 0, 4),
    ("ag", 0, 1, 2, 3), ("rp", 0), ("fp", 0, 4), ("fq", 0, 4), ("fs", 0), ("nl", 0), ("agb", 1), ("fx", 0),
    ("agp", 1), ("ag", 1, 0, 0, 0), ("ag", 1, 1, 0, 0), ("agc", 1, 0), ("ag", 1, 0, 1, 0), ("ag", 1, 1, 1, 0),
    ("fsum", 0), ("ag", 1, 0, 2, 0), ("ag", 1, 1, 2, 0), ("agc", 1, 7), ("ag", 1, 0, 0, 1), ("ag", 1, 1, 0, 1),
    ("agc", 1, 1), ("fw", 0), ("gram", 1), ("ag", 1, 1, 1, 1), ("gms", 1), ("ag", 1, 0, 1, 1), ("fp", 1, 0),
    ("fq", 1, 0), ("fp", 1, 7), ("ag", 1, 0, 2, 1), ("gp", 1), ("agc", 1, 6), ("ag", 1, 1, 2, 1), ("fq", 1, 7),
    ("cr", 1, 4), ("ag", 1, 0, 0, 2), ("ag", 1, 1, 0, 2), ("agc", 1, 2), ("cr", 1, 3), ("gz", 1), ("fp", 1, 6),
    ("fq", 1, 6), ("rs", 1, 0, 2, 0), ("rx", 1, 4), ("rs", 1, 1, 1, 0), ("cr", 1, 5), ("ag", 1, 0, 2, 2),
    ("cr", 1, 2), ("ag", 1, 1, 2, 2), ("agc", 1, 5), ("ag", 1, 1, 1, 2), ("rs", 1, 0, 1, 1), ("rx", 1, 3),
    ("fp", 1, 1), ("ag", 1, 0, 0, 3), ("agc", 1, 3), ("ag", 1, 0, 1, 2), ("fp", 1, 2), ("rs", 1, 1, 2, 1),
    ("fq", 1, 2), ("gb", 1), ("rs", 1, 1, 0, 0), ("rx", 1, 5), ("rx", 1, 2), ("cr", 1, 6), ("cr", 1, 1),
    ("rs", 1, 0, 0, 1), ("rs", 1, 0, 2, 1), ("fp", 1, 3), ("fp", 1, 5), ("rs", 1, 0, 1, 2), ("ag", 1, 1, 2, 3),
    ("agc", 1, 4), ("fq", 1, 3), ("rx", 1, 6), ("gs", 1), ("fq", 1, 5), ("rs", 1, 1, 2, 2), ("ag", 1, 0, 1, 3),
    ("rx", 1, 1), ("fq", 1, 1), ("gf", 1), ("cr", 1, 7), ("rs", 1, 1, 0, 1), ("cr", 1, 0), ("rs", 1, 0, 0, 2),
    ("fp", 1, 4), ("fq", 1, 4), ("fs", 1), ("rs", 1, 1, 1, 1), ("rs", 1, 0, 2, 2), ("rx", 1, 7),
    ("rs", 1, 1, 2, 3), ("rx", 1, 0), ("rs", 1, 0, 1, 3), ("rs", 1, 1, 0, 2), ("gy", 1), ("rs", 1, 0, 0, 3),
    ("rs", 1, 1, 1, 2), ("rs", 1, 0, 2, 3), ("fx", 1), ("rs", 1, 1, 0, 3), ("fsum", 1), ("rs", 1, 1, 1, 3),
    ("rp", 1), ("nl", 1), ("fw", 1),
)


def nn(a, b):
    return jnp.dot(a, b, preferred_element_type=F32)


def nt(a, b):
    return lax.dot_general(a, b, (((1,), (1,)), ((), ())), preferred_element_type=F32)


def kernel(
    rate_z, rate_w,
    x_hbm, z_hbm, w_hbm, mask, modality_hbm, z_out, w_out,
    x, obs, zb, zt, zf, wf, wg, own, sib_out, sib_in, ring_out, ring_in, x_out, x_in, pair_out, pair_in,
    g_local, g_sib, g_half, g_pair, g_z, g_all, pz, z_in_parts, z_sum, z_new,
    z_in, w_in, w_new, modality, x_sem, in_sem, out_sem, ag_s, ag_r, agx_s, agx_r, ags_s, ags_r, rs_s, rs_r, rsa_s, rsa_r, rsx_s, rsx_r, rss_s, rss_r,
    g_s, g_r, gz_s, gz_r, gf_s, gf_r, az_s, az_r, an_s, an_r,
):
    s = lax.axis_index("sample")
    k = lax.axis_index("feat")
    z = s // 4
    xh = (s // 2) % 2
    c = s % 2
    batch = z // 4
    xl = k // 4
    y = k % 4
    sibling = {"sample": z * 4 + xh * 2 + (1 - c)}
    partner = {"sample": z * 4 + (1 - xh) * 2 + c}

    def along(step):
        return {"sample": ((z + step + NZ) % NZ) * 4 + xh * 2 + c}

    def y_peer(off):
        return {"feat": xl * 4 + (y + off) % 4}

    x_peer = {"feat": (1 - xl) * 4 + y}

    neighbour = (along(1), along(-1))
    started = []

    def copy(src, dst, send, recv, device):
        return pltpu.make_async_remote_copy(
            src_ref=src, dst_ref=dst, send_sem=send, recv_sem=recv,
            device_id=device, device_id_type=pl.DeviceIdType.MESH,
        )

    def send(*args):
        one = copy(*args)
        one.start()
        started.append(one)

    def shard(rel_z, col, core):
        which = xh if col == 0 else 1 - xh
        return ((z + rel_z + NZ) % NZ) * 4 + which * 2 + core

    load_x = pltpu.make_async_copy(x_hbm, x, x_sem)
    loads = [
        pltpu.make_async_copy(there, here, in_sem.at[i])
        for i, (there, here) in enumerate(((w_hbm, w_in), (z_hbm, z_in), (modality_hbm, modality)))
    ]
    for one in loads:
        one.start()
    load_x.start()

    barrier = pltpu.get_barrier_semaphore()
    greet = [sibling, partner] + [along(d) for d in range(1, NZ)] + [y_peer(d) for d in (1, 2, 3)] + [x_peer]
    for device in greet:
        pl.semaphore_signal(barrier, inc=1, device_id=device, device_id_type=pl.DeviceIdType.MESH)
    loads[0].wait()
    wg[0, s] = w_in[...].astype(BF)
    loads[1].wait()
    zb[0] = z_in[...].astype(BF)
    loads[2].wait()

    waited = set()

    def once(key, copies):
        if key not in waited:
            waited.add(key)
            copies().wait_recv()

    def rows(h):
        return pl.ds(h * H, H)

    def ag_send(it, d, kind, t):
        col, h = KINDS[kind]
        block = wg.at[it, shard(-t if d == 0 else t, col, c), rows(h)]
        i = ((it * 2 + d) * 3 + kind) * 4 + t
        send(block, block, ag_s.at[i], ag_r.at[i], neighbour[d])

    def ag_sibling(it, rel, col, h):
        block = wg.at[it, shard(rel, col, c), rows(h)]
        i = ((it * NZ + rel % NZ) * 2 + col) * 2 + h
        send(block, block, ags_s.at[i], ags_r.at[i], sibling)

    def ag_across(it, rel, h):
        block = wg.at[it, shard(rel, 0, c), rows(h)]
        i = it * (NZ + 1) + (NZ if h else rel % NZ)
        send(block, block, agx_s.at[i], agx_r.at[i], partner)

    def ag_begin(it):
        for kind in (0, 1):
            for d in (0, 1):
                ag_send(it, d, kind, 0)
        ag_across(it, 0, 1)
        ag_across(it, 0, 0)
        ag_sibling(it, 0, 0, 0)
        ag_sibling(it, 0, 0, 1)

    def ag_pair(it):
        block = wg.at[it, shard(0, 1, c), rows(1)]
        i = it * (NZ + 1) + NZ
        copy(block, block, agx_s.at[i], agx_r.at[i], partner).wait_recv()
        for d in (0, 1):
            ag_send(it, d, 2, 0)
        ag_sibling(it, 0, 1, 1)

    def ag_one(it, d, kind, t):
        col, h = KINDS[kind]
        full = (d, kind) in AG_FULL
        rel = -(t + 1) if d == 0 else t + 1
        block = wg.at[it, shard(rel, col, c), rows(h)]
        i = ((it * 2 + d) * 3 + kind) * 4 + t
        copy(block, block, ag_s.at[i], ag_r.at[i], neighbour[d]).wait_recv()
        if t < 2 or (t == 2 and full):
            ag_send(it, d, kind, t + 1)
        if kind == 0:
            ag_across(it, rel, 0)
        ag_sibling(it, rel, col, h)

    def ag_crossed(it, rel):
        block = wg.at[it, shard(rel, 1, c), rows(0)]
        i = it * (NZ + 1) + rel % NZ
        copy(block, block, agx_s.at[i], agx_r.at[i], partner).wait_recv()
        ag_sibling(it, rel, 1, 0)

    def ag_from_sibling(it, rel):
        for col, h in ((0, 0), (0, 1), (1, 1), (1, 0)):
            block = wg.at[it, shard(rel, col, 1 - c), rows(h)]
            i = ((it * NZ + rel % NZ) * 2 + col) * 2 + h
            copy(block, block, ags_s.at[i], ags_r.at[i], sibling).wait_recv()

    def factor_half(it, rel, j):
        there = (z + rel + NZ) % NZ
        w = wg[it, pl.ds(there * 4 + j * 2, 2)].reshape(2 * T, T)
        cols = pl.ds(pl.multiple_of(there * 4 * T + j * 2 * T, 2 * T), 2 * T)
        pred = nt(zb[it], w)
        resid = (obs[batch, :, cols] * (pred - x[:, cols].astype(F32))).astype(BF)
        part = nn(resid, w)
        if ("pz", it) in waited:
            pz[it] += part
        else:
            pz[it] = part
        waited.add(("pz", it))

    def factor_part(it, rel):
        ag_from_sibling(it, rel)
        factor_half(it, rel, 0)

    def factor_rest(it, rel):
        factor_half(it, rel, 1)

    def cross(it, rel):
        there = (z + rel) % NZ

        def body(col, carry):
            which = (xh + col) % 2
            slot = rel * 2 + col
            for mine in (False, True):
                core = c if mine else 1 - c
                cols = pl.ds(pl.multiple_of((there * 4 + which * 2 + core) * T, T), T)
                value = nn(zt[...], x[:, cols]) * obs[batch, :, cols]
                if mine:
                    own[slot] = value
                else:
                    sib_out[it, slot] = value.astype(BF)
                    if it == 1:
                        sem = it * 2 * NZ + slot
                        copy(
                            sib_out.at[it, slot], sib_in.at[it, slot], rss_s.at[sem], rss_r.at[sem], sibling
                        ).start()
            return carry

        lax.fori_loop(0, 2, body, 0)

    def cross_send(rel):
        for col in (0, 1):
            slot = rel * 2 + col
            copy(
                sib_out.at[0, slot], sib_in.at[0, slot], rss_s.at[slot], rss_r.at[slot], sibling
            ).start()

    def cross_end(it):
        def body(slot, carry):
            sem = it * 2 * NZ + slot
            copy(
                sib_out.at[it, slot], sib_in.at[it, slot], rss_s.at[sem], rss_r.at[sem], sibling
            ).wait_send()
            return carry

        lax.fori_loop(0, 2 * NZ, body, 0)

    def chip_sum(it, rel, col, h):
        slot = (rel % NZ) * 2 + col
        sem = it * 2 * NZ + slot
        once(("sib", it, slot), lambda: copy(
            sib_out.at[it, slot], sib_in.at[it, slot], rss_s.at[sem], rss_r.at[sem], sibling
        ))
        value = own[slot, rows(h)] + sib_in[it, slot, rows(h)].astype(F32)
        if col == 0 and h == 0:
            i = it * NZ + rel % NZ
            once(("x", it, rel % NZ), lambda: copy(
                x_out.at[i], x_in.at[i], rsa_s.at[i], rsa_r.at[i], partner
            ))
            value = value + x_in[i].astype(F32)
        return value

    def rs_across(it, rel):
        i = it * NZ + rel
        x_out[i] = chip_sum(it, rel, 1, 0).astype(BF)
        send(x_out.at[i], x_in.at[i], rsa_s.at[i], rsa_r.at[i], partner)

    def arrived(it, d, kind, t):
        i = ((it * 2 + d) * 3 + kind) * 4 + t
        copy(ring_out.at[i], ring_in.at[i], rs_s.at[i], rs_r.at[i], neighbour[d]).wait_recv()
        return ring_in[i].astype(F32)

    def rs_one(it, d, kind, t):
        col, h = KINDS[kind]
        value = chip_sum(it, 4 - t if d == 0 else t - 4, col, h)
        if t > 1 or (t == 1 and (d, kind) in RS_FULL):
            value = value + arrived(it, d, kind, t - 1)
        i = ((it * 2 + d) * 3 + kind) * 4 + t
        ring_out[i] = value.astype(BF)
        send(ring_out.at[i], ring_in.at[i], rs_s.at[i], rs_r.at[i], neighbour[d])

    def rs_pair_send(it):
        value = chip_sum(it, 0, 1, 1) + arrived(it, 0, 2, 3) + arrived(it, 1, 2, 3)
        pair_out[it] = value.astype(BF)
        send(pair_out.at[it], pair_in.at[it], rsx_s.at[it], rsx_r.at[it], partner)

    def rs_end(it):
        low = chip_sum(it, 0, 0, 0) + arrived(it, 0, 0, 3) + arrived(it, 1, 0, 3)
        high = chip_sum(it, 0, 0, 1) + arrived(it, 0, 1, 3) + arrived(it, 1, 1, 3)
        copy(pair_out.at[it], pair_in.at[it], rsx_s.at[it], rsx_r.at[it], partner).wait_recv()
        return jnp.concatenate([low, high + pair_in[it].astype(F32)], axis=0)

    rows64 = pl.multiple_of(y * 64, 64)

    kk = y * 2 + xl
    half = pl.multiple_of(kk * 32 + c * 16, 16)
    other_half = pl.multiple_of(kk * 32 + (1 - c) * 16, 16)
    base = pl.multiple_of(kk * 32 + c * 16 + xh * 8, 8)
    mine8 = pl.multiple_of(xh * 8, 8)
    other8 = pl.multiple_of((1 - xh) * 8, 8)

    def gram(it):
        zt[...] = zb[it].astype(F32).T.astype(BF)
        g_local[it] = nn(zt[...], zb[it])

    def gram_send(it):
        i = it * 4
        send(g_local.at[it, pl.ds(other_half, 16)], g_sib.at[it], g_s.at[i], g_r.at[i], sibling)

    def gram_pair(it):
        i = it * 4
        copy(g_half.at[it], g_sib.at[it], g_s.at[i], g_r.at[i], sibling).wait_recv()
        g_half[it] = g_local[it, pl.ds(half, 16)] + g_sib[it]
        i = it * 4 + 1
        send(g_half.at[it, pl.ds(other8, 8)], g_pair.at[it], g_s.at[i], g_r.at[i], partner)

    def gram_z(it):
        i = it * 4 + 1
        copy(g_pair.at[it], g_pair.at[it], g_s.at[i], g_r.at[i], partner).wait_recv()
        g_z[it, z] = g_half[it, pl.ds(mine8, 8)] + g_pair[it]
        for off in range(1, NZ):
            i = it * NZ + off
            send(g_z.at[it, z], g_z.at[it, z], gz_s.at[i], gz_r.at[i], along(off))

    def gram_batches(it):
        for off in range(1, NZ):
            i = it * NZ + off
            slot = g_z.at[it, (z + NZ - off) % NZ]
            copy(slot, slot, gz_s.at[i], gz_r.at[i], along(off)).wait_recv()
        for b in (0, 1):
            g_all[it, b, pl.ds(base, 8)] = (
                (g_z[it, 4 * b] + g_z[it, 4 * b + 1]) + (g_z[it, 4 * b + 2] + g_z[it, 4 * b + 3])
            )
        block = g_all.at[it, :, pl.ds(base, 8)]
        send(block, block, g_s.at[it * 4 + 2], g_r.at[it * 4 + 2], partner)

    def gram_sibling(it):
        rows = pl.multiple_of(kk * 32 + c * 16 + (1 - xh) * 8, 8)
        block = g_all.at[it, :, pl.ds(rows, 8)]
        copy(block, block, g_s.at[it * 4 + 2], g_r.at[it * 4 + 2], partner).wait_recv()
        block = g_all.at[it, :, pl.ds(half, 16)]
        send(block, block, g_s.at[it * 4 + 3], g_r.at[it * 4 + 3], sibling)

    def gram_feat(it):
        block = g_all.at[it, :, pl.ds(other_half, 16)]
        copy(block, block, g_s.at[it * 4 + 3], g_r.at[it * 4 + 3], sibling).wait_recv()
        block = g_all.at[it, :, pl.ds(pl.multiple_of(kk * 32, 32), 32)]
        send(block, block, gf_s.at[it * 4], gf_r.at[it * 4], x_peer)

    def gram_y(it):
        block = g_all.at[it, :, pl.ds(pl.multiple_of(y * 64 + (1 - xl) * 32, 32), 32)]
        copy(block, block, gf_s.at[it * 4], gf_r.at[it * 4], x_peer).wait_recv()
        block = g_all.at[it, :, pl.ds(rows64, 64)]
        for off in (1, 2, 3):
            i = it * 4 + off
            send(block, block, gf_s.at[i], gf_r.at[i], y_peer(off))

    def new_loadings(it):
        for off in (1, 2, 3):
            i = it * 4 + off
            block = g_all.at[it, :, pl.ds(pl.multiple_of(((y + 4 - off) % 4) * 64, 64), 64)]
            copy(block, block, gf_s.at[i], gf_r.at[i], y_peer(off)).wait_recv()
        cols = pl.ds(pl.multiple_of(s * T, T), T)
        w = wg[it, s]
        grad = jnp.zeros((T, T), F32)
        for b in (0, 1):
            g = g_all[it, b]
            high = g.astype(BF)
            low = (g - high.astype(F32)).astype(BF)
            grad = grad + obs[b, :, cols] * (nt(high, w) + nt(low, w))
        grad = grad - rs_end(it)
        new = (w_in[...] if it == 0 else wf[...]) - rate_w * grad.T
        if it == 0:
            wf[...] = new
            wg[1, s] = new.astype(BF)
        else:
            w_new[...] = new
            pltpu.make_async_copy(w_new, w_out, out_sem.at[0]).start()

    def factors_send(it):
        for off in (1, 2, 3):
            i = it * 4 + off
            there = pl.multiple_of(((y + off) % 4) * 64, 64)
            send(pz.at[it, pl.ds(there, 64)], z_in_parts.at[it, off], az_s.at[i], az_r.at[i], y_peer(off))

    def factors_across(it):
        total = pz[it, pl.ds(rows64, 64)]
        for off in (1, 2, 3):
            i = it * 4 + off
            slot = z_in_parts.at[it, off]
            copy(slot, slot, az_s.at[i], az_r.at[i], y_peer(off)).wait_recv()
            total = total + z_in_parts[it, off]
        z_sum[it, 0] = total
        send(z_sum.at[it, 0], z_sum.at[it, 1], az_s.at[it * 4], az_r.at[it * 4], x_peer)

    def factors_sum(it):
        copy(z_sum.at[it, 0], z_sum.at[it, 1], az_s.at[it * 4], az_r.at[it * 4], x_peer).wait_recv()
        old = z_in[pl.ds(rows64, 64)] if it == 0 else zf[...]
        new = old - rate_z * (z_sum[it, 0] + z_sum[it, 1])
        if it == 0:
            zf[...] = new
            zb[1, pl.ds(rows64, 64)] = new.astype(BF)
        else:
            z_new[pl.ds(rows64, 64)] = new
        target = zb.at[1] if it == 0 else z_new
        block = target.at[pl.ds(rows64, 64)]
        for off in (1, 2, 3):
            i = it * 4 + off
            send(block, block, an_s.at[i], an_r.at[i], y_peer(off))

    def factors_wait(it):
        target = zb.at[1] if it == 0 else z_new
        for off in (1, 2, 3):
            i = it * 4 + off
            block = target.at[pl.ds(pl.multiple_of(((y + 4 - off) % 4) * 64, 64), 64)]
            copy(block, block, an_s.at[i], an_r.at[i], y_peer(off)).wait_recv()
        if it == 1:
            pltpu.make_async_copy(z_new, z_out, out_sem.at[1]).start()

    def enter():
        pl.semaphore_wait(barrier, len(greet))

    def load():
        for b in (0, 1):
            seen = jnp.zeros(modality.shape, F32)
            for m in range(MODS):
                seen = jnp.where(modality[...] == m, mask[b, m].astype(F32), seen)
            obs[b] = seen
        load_x.wait()

    do = {
        "agb": ag_begin, "agp": ag_pair, "ag": ag_one, "agc": ag_crossed, "fp": factor_part, "fq": factor_rest,
        "fs": factors_send, "fsum": factors_sum, "fw": factors_wait,
        "gram": gram, "gp": gram_pair, "gz": gram_z, "gb": gram_batches, "gs": gram_sibling, "gf": gram_feat,
        "cr": cross, "rx": rs_across, "rs": rs_one, "rp": rs_pair_send, "nl": new_loadings, "ld": load,
        "bar": enter, "crs": cross_send, "gms": gram_send, "gy": gram_y, "fx": factors_across,
    }
    marks = []
    ended = 0
    for step, (name, *where) in enumerate(ORDER):
        do[name](*where)
        marks.append(len(started))
        if step >= 40:
            for one in started[ended:marks[step - 40]]:
                one.wait_send()
            ended = marks[step - 40]
        if (name, where) == ("agb", [1]):
            cross_end(0)
    for one in started[ended:]:
        one.wait_send()
    cross_end(1)
    pltpu.make_async_copy(w_new, w_out, out_sem.at[0]).wait()
    pltpu.make_async_copy(z_new, z_out, out_sem.at[1]).wait()


def hand_over(z_from, w_from, z_to, w_to):
    z_to[...] = z_from[...]
    w_to[...] = w_from[...]


def per_device(expression, factors, loadings, batch_mask, modality):
    rows = factors.shape[0]
    rank = factors.shape[1]
    cells = rows * lax.axis_size("sample")
    width = expression.shape[1]
    features = width * lax.axis_size("feat")
    rate_z = 0.9 * math.sqrt(rank) / features
    rate_w = 0.9 * math.sqrt(rank) / cells
    hbm = pl.BlockSpec(memory_space=pl.ANY)
    vm = pl.BlockSpec(memory_space=pltpu.VMEM)
    dma = lambda n: pltpu.SemaphoreType.DMA((n,))
    out = jax.ShapeDtypeStruct((T, T), F32)

    def body(*refs):
        kernel(rate_z, rate_w, *refs)

    z_out, w_out = pl.pallas_call(
        body,
        out_shape=(out, out),
        in_specs=[
            hbm, hbm, hbm, pl.BlockSpec(memory_space=pltpu.SMEM), hbm,
        ],
        out_specs=(hbm, hbm),
        scratch_shapes=[
            pltpu.VMEM((rows, width), BF),
            pltpu.VMEM((2, 1, width), F32),
            pltpu.VMEM((ITERS, T, T), BF),
            pltpu.VMEM((T, T), BF),
            pltpu.VMEM((64, T), F32),
            pltpu.VMEM((T, T), F32),
            pltpu.VMEM((ITERS, 32, T, T), BF),
            pltpu.VMEM((2 * NZ, T, T), F32),
            pltpu.VMEM((ITERS, 2 * NZ, T, T), BF),
            pltpu.VMEM((ITERS, 2 * NZ, T, T), BF),
            pltpu.VMEM((ITERS * 24, H, T), BF),
            pltpu.VMEM((ITERS * 24, H, T), BF),
            pltpu.VMEM((ITERS * NZ, H, T), BF),
            pltpu.VMEM((ITERS * NZ, H, T), BF),
            pltpu.VMEM((ITERS, H, T), BF),
            pltpu.VMEM((ITERS, H, T), BF),
            pltpu.VMEM((ITERS, T, T), F32),
            pltpu.VMEM((ITERS, 16, T), F32),
            pltpu.VMEM((ITERS, 16, T), F32),
            pltpu.VMEM((ITERS, 8, T), F32),
            pltpu.VMEM((ITERS, NZ, 8, T), F32),
            pltpu.VMEM((ITERS, 2, T, T), F32),
            pltpu.VMEM((ITERS, T, T), F32),
            pltpu.VMEM((ITERS, 4, 64, T), F32),
            pltpu.VMEM((ITERS, 2, 64, T), F32),
            pltpu.VMEM((T, T), F32),
            pltpu.VMEM((T, T), F32),
            pltpu.VMEM((T, T), F32),
            pltpu.VMEM((T, T), F32),
            pltpu.VMEM((1, width), jnp.int32),
            pltpu.SemaphoreType.DMA,
            dma(3), dma(2),
            dma(ITERS * 24), dma(ITERS * 24),
            dma(ITERS * (NZ + 1)), dma(ITERS * (NZ + 1)),
            dma(ITERS * 32), dma(ITERS * 32),
            dma(ITERS * 24), dma(ITERS * 24),
            dma(ITERS * NZ), dma(ITERS * NZ),
            dma(ITERS), dma(ITERS),
            dma(ITERS * 16), dma(ITERS * 16),
            dma(ITERS * 4), dma(ITERS * 4),
            dma(ITERS * NZ), dma(ITERS * NZ),
            dma(ITERS * 4), dma(ITERS * 4),
            dma(ITERS * 4), dma(ITERS * 4),
            dma(ITERS * 4), dma(ITERS * 4),
        ],
        compiler_params=pltpu.CompilerParams(
            collective_id=0, has_side_effects=True, vmem_limit_bytes=60 * 1024 * 1024
        ),
    )(expression, factors, loadings, batch_mask, modality.reshape(1, width))
    return pl.pallas_call(
        hand_over,
        out_shape=(out, out),
        in_specs=[vm, vm],
        out_specs=(vm, vm),
    )(z_out, w_out)


def solution(mesh):
    return jax.shard_map(
        per_device,
        mesh=mesh,
        in_specs=(
            P("sample", "feat"),
            P("sample", None),
            P(("feat", "sample"), None),
            P(),
            P("feat"),
        ),
        out_specs=(P("sample", None), P(("feat", "sample"), None)),
        check_vma=False,
    )
```
